32 devices in a mesh: parts: 2 (over x), harm: 4 (over y, core), tile: 4 (over z).
Axes of the slice: x: 2, y: 2, z: 4, core: 2. Of those that a mesh axis runs over, the one named last changes fastest.
Arguments:
- perturbation: float32 [8, 2, 5, 128, 256], P('harm', None, None, ('parts', 'tile')), parts along dimension 3, may hold values from -6 to 6
- base_flow: float32 [8, 2, 3, 128, 256], P('harm', None, None, ('parts', 'tile')), parts along dimension 3, may hold values from -0.9 to 0.9
- viscosity: float32 [128, 256], P(('parts', 'tile')), parts along dimension 0, may hold values from 0.05 to 0.5
Outputs:
- resolvent_image: float32 [8, 2, 5, 128, 256], P('harm', None, None, ('parts', 'tile')), parts along dimension 3
The draws below stay inside these ranges and needn't reach their ends.
There are 2 independent parts, one for each index of `parts`. The reference program is written for one: setup_inputs(seed, part) draws one part's arguments, and reference() takes and returns one part's arrays. A program takes and returns all parts, laid end to end along the dimension named above; each array names one. Nothing has to cross between parts.
All inputs are finite; a program needn't handle non-finite values.
Results may differ from the reference program's by a relative error of at most 0.00002.
Values sent between devices are 32-bit elements; how exact they have to be, the bound alone decides.
No kernel may reach another device: no remote copies, remote signals or barrier semaphores. Data moves between devices by JAX's collectives and lax.ppermute only.
A program may use at most 64 MiB of HBM per device.

```python
import math
import jax
import jax.numpy as jnp
from jax import lax

FIELDS = 5
CY = 256
NH = 8
NXG = 64


def shard_levels(stream_key, dims, split, smallest, high):
    level, own = 1.0, jax.random.fold_in(stream_key, 6)
    for axis_at, parts in split:
        steps = jnp.exp(jax.random.uniform(jax.random.fold_in(own, axis_at), (parts,), jnp.float32, smallest / len(split), high / len(split)))
        level = level * jnp.repeat(steps, dims[axis_at] // parts).reshape([-1 if axis == axis_at else 1 for axis in range(len(dims))])
    return level


def scatter_about(own_key, dims, width, limit, shards=(), kind=jnp.bfloat16):
    drawn = width * jax.random.normal(own_key, dims, jnp.float32)
    if shards:
        drawn = drawn * shard_levels(own_key, dims, shards, -0.22, 0.18)
    return jnp.clip(drawn, -limit, limit).astype(kind)


def setup_inputs(seed: int = 0, part: int = 0) -> dict:
    streams_of = jax.random.split(jax.random.key(seed), 4)
    part_keys = jax.random.split(jax.random.fold_in(streams_of[3], part), 4)
    return {
        "perturbation": scatter_about(part_keys[0], (NH, 2, FIELDS, NXG, CY), 1.0, 6.0, ((0, 4), (3, 4)), jnp.float32),
        "base_flow": scatter_about(part_keys[1], (NH, 2, 3, NXG, CY), 0.15, 0.9, ((0, 4), (3, 4)), jnp.float32),
        "viscosity": jnp.clip(jnp.exp(math.log(0.5) - 2.3025851 * jax.random.uniform(part_keys[2], (NXG, CY), jnp.float32) ** shard_levels(part_keys[2], (NXG, CY), ((0, 4),), -0.2, 0.2)), 0.05, 0.5),
    }


omega_base = 0.25


def along_first(values):
    return 0.5 * (jnp.roll(values, -1, -2) - jnp.roll(values, 1, -2))


def along_second(values):
    return 0.5 * (jnp.roll(values, -1, -1) - jnp.roll(values, 1, -1))


def diffusion(values, viscosity):
    east_face = 0.5 * (viscosity + jnp.roll(viscosity, -1, -2))
    west_face = 0.5 * (viscosity + jnp.roll(viscosity, 1, -2))
    north_face = 0.5 * (viscosity + jnp.roll(viscosity, -1, -1))
    south_face = 0.5 * (viscosity + jnp.roll(viscosity, 1, -1))
    return (east_face * (jnp.roll(values, -1, -2) - values) - west_face * (values - jnp.roll(values, 1, -2))
            + north_face * (jnp.roll(values, -1, -1) - values) - south_face * (values - jnp.roll(values, 1, -1)))


def acoustic(grad_x, grad_y):
    dilation = grad_x[..., 1, :, :] + grad_y[..., 2, :, :]
    return jnp.stack([dilation, grad_x[..., 4, :, :], grad_y[..., 4, :, :], jnp.zeros_like(dilation), dilation], axis=-3)


def own_terms(middle, grad_x, grad_y, damping, frequency):
    rotation = jnp.stack([-frequency * middle[:, 1], frequency * middle[:, 0]], axis=1)
    return rotation + acoustic(grad_x, grad_y) - damping


def coupling(u_real, u_imag, v_real, v_imag, g_real, g_imag, q_real, q_imag, x_real, x_imag, y_real, y_imag):
    real_part = u_real * x_real - u_imag * x_imag + v_real * y_real - v_imag * y_imag + g_real * q_real - g_imag * q_imag
    imag_part = u_real * x_imag + u_imag * x_real + v_real * y_imag + v_imag * y_real + g_real * q_imag + g_imag * q_real
    return real_part, imag_part


def reference(perturbation, base_flow, viscosity):
    grad_x = along_first(perturbation)
    grad_y = along_second(perturbation)
    numbers = jnp.arange(NH, dtype=jnp.int32)
    signed = jnp.where(numbers < NH // 2, numbers, numbers - NH)
    frequency = (omega_base * signed.astype(jnp.float32)).reshape(NH, 1, 1, 1)
    summed = own_terms(perturbation, grad_x, grad_y, diffusion(perturbation, viscosity), frequency)

    def add_source(source, summed):
        shifted = jnp.roll(base_flow, source, axis=0)
        values = lax.dynamic_index_in_dim(perturbation, source, 0, keepdims=False)
        slope_x = lax.dynamic_index_in_dim(grad_x, source, 0, keepdims=False)
        slope_y = lax.dynamic_index_in_dim(grad_y, source, 0, keepdims=False)
        real_part, imag_part = coupling(
            shifted[:, 0, 0][:, None], shifted[:, 1, 0][:, None],
            shifted[:, 0, 1][:, None], shifted[:, 1, 1][:, None],
            shifted[:, 0, 2][:, None], shifted[:, 1, 2][:, None],
            values[0], values[1], slope_x[0], slope_x[1], slope_y[0], slope_y[1])
        return summed + jnp.stack([real_part, imag_part], axis=1)

    summed = lax.fori_loop(0, NH, add_source, summed)
    return summed
```

```python
import functools

import jax
import jax.numpy as jnp
import numpy as np
from jax import lax
from jax.experimental import pallas as pl
from jax.experimental.pallas import tpu as pltpu
from jax.sharding import PartitionSpec as P

omega_base = 0.25


def extended(cells, sides, width):
    for axis, dim in sides:
        count = lax.axis_size(axis)
        head = lax.slice_in_dim(cells, 0, width, axis=dim)
        tail = lax.slice_in_dim(cells, cells.shape[dim] - width, cells.shape[dim], axis=dim)
        cells = jnp.concatenate(
            [
                lax.ppermute(tail, axis, [(i, (i + 1) % count) for i in range(count)]),
                cells,
                lax.ppermute(head, axis, [((i + 1) % count, i) for i in range(count)]),
            ],
            axis=dim,
        )
    return cells


def shifted(value, axis, steps):
    count = lax.axis_size(axis)
    pairs = [(source, (source + steps) % count) for source in range(count)]
    return lax.ppermute(value, axis, pairs)


def split_rows(padded):
    middle = padded[..., 1:-1, :]
    grad_x = 0.5 * (padded[..., 2:, :] - padded[..., :-2, :])
    grad_y = 0.5 * (jnp.roll(middle, -1, -1) - jnp.roll(middle, 1, -1))
    return (middle, grad_x, grad_y)


def diffusion(padded, visc_padded):
    middle = padded[..., 1:-1, :]
    center = visc_padded[1:-1]
    east_face = 0.5 * (center + visc_padded[2:])
    west_face = 0.5 * (center + visc_padded[:-2])
    north_face = 0.5 * (center + jnp.roll(center, -1, -1))
    south_face = 0.5 * (center + jnp.roll(center, 1, -1))
    return (
        east_face * (padded[..., 2:, :] - middle)
        - west_face * (middle - padded[..., :-2, :])
        + north_face * (jnp.roll(middle, -1, -1) - middle)
        - south_face * (middle - jnp.roll(middle, 1, -1))
    )


def acoustic(grad_x, grad_y):
    dilation = grad_x[..., 1, :, :] + grad_y[..., 2, :, :]
    return jnp.stack(
        [dilation, grad_x[..., 4, :, :], grad_y[..., 4, :, :], jnp.zeros_like(dilation), dilation],
        axis=-3,
    )


def own_terms(middle, grad_x, grad_y, damping, frequency):
    rotation = jnp.stack([-frequency * middle[:, 1], frequency * middle[:, 0]], axis=1)
    return rotation + acoustic(grad_x, grad_y) - damping


def coupling(
    u_real, u_imag, v_real, v_imag, g_real, g_imag, q_real, q_imag, x_real, x_imag, y_real, y_imag
):
    real_part = (
        u_real * x_real
        - u_imag * x_imag
        + v_real * y_real
        - v_imag * y_imag
        + g_real * q_real
        - g_imag * q_imag
    )
    imag_part = (
        u_real * x_imag
        + u_imag * x_real
        + v_real * y_imag
        + v_imag * y_real
        + g_real * q_imag
        + g_imag * q_real
    )
    return (real_part, imag_part)


def block_terms(blocks, middle, grad_x, grad_y):
    local_count = middle.shape[0]
    index_table = np.array(
        [
            [local_count + target - source for source in range(local_count)]
            for target in range(local_count)
        ],
        dtype=np.int32,
    )
    chosen = blocks[index_table]

    def base_part(complex_index, field_index):
        return chosen[:, :, complex_index, field_index][:, :, None]

    def moved_part(values, complex_index):
        return values[None, :, complex_index]

    real_part, imag_part = coupling(
        base_part(0, 0),
        base_part(1, 0),
        base_part(0, 1),
        base_part(1, 1),
        base_part(0, 2),
        base_part(1, 2),
        moved_part(middle, 0),
        moved_part(middle, 1),
        moved_part(grad_x, 0),
        moved_part(grad_x, 1),
        moved_part(grad_y, 0),
        moved_part(grad_y, 1),
    )
    return jnp.stack([jnp.sum(real_part, axis=1), jnp.sum(imag_part, axis=1)], axis=1)


def shards(perturbation, base_flow, viscosity):
    local_count = perturbation.shape[0]
    width_x = perturbation.shape[3]
    width_y = perturbation.shape[4]
    groups = lax.axis_size("harm")
    first_index = lax.axis_index("harm") * local_count
    flattened = perturbation.reshape(local_count * 10, width_x, width_y)
    stacked = jnp.concatenate([flattened, viscosity[None]], axis=0)
    padded = extended(stacked, (("tile", 1),), 1)
    own_padded = padded[:-1].reshape(local_count, 2, 5, width_x + 2, width_y)
    visc_padded = padded[-1]
    numbers = first_index + jnp.arange(local_count, dtype=jnp.int32)
    total_count = local_count * groups
    signed = jnp.where(numbers < total_count // 2, numbers, numbers - total_count)
    frequency = (omega_base * signed.astype(jnp.float32)).reshape(local_count, 1, 1, 1)
    middle, grad_x, grad_y = split_rows(own_padded)
    summed = own_terms(middle, grad_x, grad_y, diffusion(own_padded, visc_padded), frequency)
    whole_base = lax.all_gather(base_flow, "harm", axis=0, tiled=True)

    def base_pair(position, earlier):
        before = lax.dynamic_slice_in_dim(
            whole_base, (position + groups - 1) % groups * local_count, local_count, 0
        )
        current = lax.dynamic_slice_in_dim(whole_base, position * local_count, local_count, 0)
        return (jnp.concatenate([before, current], axis=0), earlier)

    earlier = base_flow
    moving = own_padded

    def advance(moving):
        moved = shifted(moving, "harm", 1)
        return (moved, moved)

    blocks, earlier = base_pair(0, earlier)
    summed = summed + block_terms(blocks, middle, grad_x, grad_y)

    def advance_step(position, carried):
        summed, moving, earlier = carried
        moving, rimmed = advance(moving)
        blocks, earlier = base_pair(position, earlier)
        values, slope_x, slope_y = split_rows(rimmed)
        return (summed + block_terms(blocks, values, slope_x, slope_y), moving, earlier)

    summed, moving, earlier = lax.fori_loop(1, groups, advance_step, (summed, moving, earlier))
    return summed


def ceil_to(count, unit):
    return -(-count // unit) * unit


def block_call(kernel, outs, scratch=()):
    shapes = [jax.ShapeDtypeStruct(shape, jnp.float32) for shape in outs]
    return pl.pallas_call(
        kernel,
        out_shape=shapes,
        out_specs=[pl.BlockSpec(memory_space=pltpu.VMEM)] * len(outs),
        scratch_shapes=[pltpu.VMEM(shape, jnp.float32) for shape in scratch],
    )


def lanes_next(value):
    return pltpu.roll(value, value.shape[1] - 1, 1)


def lanes_before(value):
    return pltpu.roll(value, 1, 1)


def rows_next(value, below):
    count = value.shape[0]
    row = lax.broadcasted_iota(jnp.int32, value.shape, 0)
    return jnp.where(row == count - 1, below, pltpu.roll(value, count - 1, 0))


def rows_before(value, above):
    row = lax.broadcasted_iota(jnp.int32, value.shape, 0)
    return jnp.where(row == 0, above, pltpu.roll(value, 1, 0))


class Sizes:
    def __init__(self, perturbation, groups):
        self.local, _, self.fields, self.width, self.columns = perturbation.shape
        self.groups = groups
        self.half = self.width // 2
        self.total = self.local * groups
        self.components = self.local * 2 * self.fields
        self.edge = ceil_to(self.components + 1, 8)
        cut = self.fields // 2
        self.chunks = ((0, cut), (cut, self.fields))

    def at(self, harmonic, part, field):
        return (harmonic * 2 + part) * self.fields + field

    def block(self, chunk, harmonic, part, field):
        first, last = self.chunks[chunk]
        start = ((harmonic * 2 + part) * (last - first) + field - first) * self.half
        return slice(start, start + self.half)

    def block_rows(self, chunk):
        first, last = self.chunks[chunk]
        return self.local * 2 * (last - first) * self.half

    def each(self, fields=None):
        for harmonic in range(self.local):
            for part in range(2):
                for field in fields if fields is not None else range(self.fields):
                    yield harmonic, part, field


def pack_kernel(sizes, q_ref, visc_ref, first_ref, second_ref, outer_ref, other_ref):
    chip = lax.axis_index("harm") // 2
    lower = chip == 0
    far = pl.multiple_of((1 - chip) * sizes.half, sizes.half)
    last, half = sizes.width - 1, sizes.half
    messages = (first_ref, second_ref)
    inner_at = sizes.block_rows(0)
    for harmonic, part, field in sizes.each():
        chunk = 0 if field < sizes.chunks[0][1] else 1
        value = q_ref[harmonic, part, field, pl.ds(far, half), :]
        messages[chunk][sizes.block(chunk, harmonic, part, field), :] = value
        at = sizes.at(harmonic, part, field)
        top = q_ref[harmonic, part, field, 0:1, :]
        bottom = q_ref[harmonic, part, field, last : last + 1, :]
        outer_ref[at : at + 1, :] = jnp.where(lower, bottom, top)
        other_ref[at : at + 1, :] = jnp.where(lower, top, bottom)
        above = q_ref[harmonic, part, field, half - 1 : half, :]
        below = q_ref[harmonic, part, field, half : half + 1, :]
        first_ref[inner_at + at : inner_at + at + 1, :] = jnp.where(lower, above, below)
    at = sizes.components
    top, bottom = visc_ref[0:1, :], visc_ref[last : last + 1, :]
    outer_ref[at : at + 1, :] = jnp.where(lower, bottom, top)
    other_ref[at : at + 1, :] = jnp.where(lower, top, bottom)
    spare = jnp.zeros((sizes.edge - at - 1, sizes.columns), jnp.float32)
    outer_ref[at + 1 :, :] = spare
    other_ref[at + 1 :, :] = spare
    first_ref[inner_at + at :, :] = jnp.zeros((sizes.edge - at, sizes.columns), jnp.float32)


def own_kernel(sizes, q_ref, visc_ref, outer_ref, other_ref, sum_ref):
    me = lax.axis_index("harm")
    lower = me // 2 == 0

    def neighbours(value, at):
        outer, other = outer_ref[at : at + 1, :], other_ref[at : at + 1, :]
        above, below = jnp.where(lower, outer, other), jnp.where(lower, other, outer)
        return rows_next(value, below), rows_before(value, above)

    center = visc_ref[...]
    east_visc, west_visc = neighbours(center, sizes.components)
    east, west = 0.5 * (center + east_visc), 0.5 * (center + west_visc)
    north = 0.5 * (center + lanes_next(center))
    south = 0.5 * (center + lanes_before(center))
    for harmonic in range(sizes.local):
        number = me * sizes.local + harmonic
        signed = jnp.where(number < sizes.total // 2, number, number - sizes.total)
        frequency = omega_base * signed.astype(jnp.float32)
        for part in range(2):
            terms = {}
            for field in range(sizes.fields):
                value = q_ref[harmonic, part, field]
                x_next, x_before = neighbours(value, sizes.at(harmonic, part, field))
                y_next, y_before = lanes_next(value), lanes_before(value)
                damping = (
                    east * (x_next - value)
                    - west * (value - x_before)
                    + north * (y_next - value)
                    - south * (value - y_before)
                )
                turned = q_ref[harmonic, 1 - part, field]
                turn = -frequency if part == 0 else frequency
                terms[field] = turn * turned - damping
                if field == 1:
                    dilation = 0.5 * (x_next - x_before)
                elif field == 2:
                    dilation = dilation + 0.5 * (y_next - y_before)
                elif field == 4:
                    terms[1] = terms[1] + 0.5 * (x_next - x_before)
                    terms[2] = terms[2] + 0.5 * (y_next - y_before)
            terms[0] = terms[0] + dilation
            terms[4] = terms[4] + dilation
            for field in range(sizes.fields):
                sum_ref[harmonic, part, field] = terms[field]


def couple_kernel(sizes, chunk, *refs):
    base_refs, (q_own, q_sib), message_refs = refs[0:4], refs[4:6], refs[6:8]
    inner_refs, outer_refs = refs[8:10], refs[10:14]
    own_ref, back_ref, base, values, slopes_x, slopes_y = refs[14:]
    me = lax.axis_index("harm")
    chip = me // 2
    lower = chip == 0
    half, total = sizes.half, sizes.total
    near = pl.multiple_of(chip * half, half)
    first, last = sizes.chunks[chunk]
    inner_at = sizes.block_rows(0)
    for place in range(4):
        group = lax.bitwise_xor(me, place)
        rows = pl.ds(near, half) if place < 2 else slice(0, half)
        for harmonic in range(sizes.local):
            number = group * sizes.local + harmonic
            for part in range(2):
                for field in range(3):
                    base[number, part, field] = base_refs[place][harmonic, part, field, rows, :]
                for field in range(first, last):
                    at = sizes.at(harmonic, part, field)
                    outer = outer_refs[place][at : at + 1, :]
                    if place < 2:
                        source = (q_own, q_sib)[place]
                        value = source[harmonic, part, field, rows, :]
                        inner = jnp.where(
                            lower,
                            source[harmonic, part, field, half : half + 1, :],
                            source[harmonic, part, field, half - 1 : half, :],
                        )
                    else:
                        value = message_refs[place - 2][
                            sizes.block(chunk, harmonic, part, field), :
                        ]
                        inner = inner_refs[place - 2][inner_at + at : inner_at + at + 1, :]
                    above = jnp.where(lower, outer, inner)
                    below = jnp.where(lower, inner, outer)
                    values[number, part, field - first] = value
                    slopes_x[number, part, field - first] = 0.5 * (
                        rows_next(value, below) - rows_before(value, above)
                    )
                    slopes_y[number, part, field - first] = 0.5 * (
                        lanes_next(value) - lanes_before(value)
                    )
    targets = []
    for place, ref in ((0, own_ref), (2, back_ref)):
        for harmonic in range(sizes.local):
            number = lax.bitwise_xor(me, place) * sizes.local + harmonic
            targets.append((number, ref, harmonic))
    for field in range(last - first):
        sums = [None] * len(targets)
        for source in range(total):
            moved = [
                ref[source, part, field] for ref in (slopes_x, slopes_y, values) for part in (0, 1)
            ]
            for place, (number, _, _) in enumerate(targets):
                at = lax.rem(number - source + total, total)
                chosen = [base[at, part, term] for term in range(3) for part in (0, 1)]
                real = imag = None
                for term in range(3):
                    c_real, c_imag = chosen[2 * term : 2 * term + 2]
                    m_real, m_imag = moved[2 * term : 2 * term + 2]
                    more_real = c_real * m_real - c_imag * m_imag
                    more_imag = c_real * m_imag + c_imag * m_real
                    real = more_real if real is None else real + more_real
                    imag = more_imag if imag is None else imag + more_imag
                if sums[place] is not None:
                    real, imag = sums[place][0] + real, sums[place][1] + imag
                sums[place] = (real, imag)
        for (_, ref, harmonic), (real, imag) in zip(targets, sums, strict=True):
            ref[harmonic, 0, field] = real
            ref[harmonic, 1, field] = imag


def join_kernel(sizes, sum_ref, *refs):
    out_ref = refs[-1]
    chip = lax.axis_index("harm") // 2
    near = pl.multiple_of(chip * sizes.half, sizes.half)
    far = pl.multiple_of((1 - chip) * sizes.half, sizes.half)
    for chunk, (first, last) in enumerate(sizes.chunks):
        for harmonic, part, field in sizes.each(range(first, last)):
            for rows, ref in ((near, refs[2 * chunk]), (far, refs[2 * chunk + 1])):
                where = (harmonic, part, field, pl.ds(rows, sizes.half), slice(None))
                out_ref[where] = sum_ref[where] + ref[harmonic, part, field - first]


def paired_shards(perturbation, base_flow, viscosity):
    groups, tiles = lax.axis_size("harm"), lax.axis_size("tile")
    sizes = Sizes(perturbation, groups)
    me = lax.axis_index("harm")
    chip = me // 2

    def to_chip(value):
        return lax.ppermute(value, "harm", [(i, i ^ 2) for i in range(groups)])

    def to_core(value):
        return lax.ppermute(value, "harm", [(i, i ^ 1) for i in range(groups)])

    def along_tile(value, steps, across):
        pairs = []
        for group in range(groups):
            step = steps[group // 2]
            for tile in range(tiles):
                target = (group ^ 2 if across else group) * tiles + (tile + step) % tiles
                pairs.append((group * tiles + tile, target))
        return lax.ppermute(value, ("harm", "tile"), pairs)

    base_half = lax.dynamic_slice_in_dim(base_flow, (1 - chip) * sizes.half, sizes.half, 3)
    base_chip = to_chip(base_half)
    base_core = to_core(base_flow)
    q_core = to_core(perturbation)

    rows = sizes.block_rows
    first, second, outer, other = block_call(
        functools.partial(pack_kernel, sizes),
        [
            (rows(0) + sizes.edge, sizes.columns),
            (rows(1), sizes.columns),
            (sizes.edge, sizes.columns),
            (sizes.edge, sizes.columns),
        ],
    )(perturbation, viscosity)
    first_chip = to_chip(first)
    outer_chip = along_tile(other, (-1, 1), True)
    outer_own = along_tile(outer, (1, -1), False)
    other_own = along_tile(other, (-1, 1), False)
    second_chip = to_chip(second)
    base_diag = to_core(base_chip)
    outer_core = to_core(outer_own)
    outer_diag = to_core(outer_chip)
    first_diag = to_core(first_chip)
    second_diag = to_core(second_chip)

    own = block_call(functools.partial(own_kernel, sizes), [perturbation.shape])(
        perturbation, viscosity, outer_own, other_own
    )[0]
    parts = []
    messages = ((first_chip, first_diag), (second_chip, second_diag))
    for chunk, (begin, end) in enumerate(sizes.chunks):
        shape = (sizes.local, 2, end - begin, sizes.half, sizes.columns)
        moved = (sizes.total, 2, end - begin, sizes.half, sizes.columns)
        kept, back = block_call(
            functools.partial(couple_kernel, sizes, chunk),
            [shape, shape],
            [(sizes.total, 2, 3, sizes.half, sizes.columns), moved, moved, moved],
        )(
            base_flow,
            base_core,
            base_chip,
            base_diag,
            perturbation,
            q_core,
            *messages[chunk],
            first_chip,
            first_diag,
            outer_own,
            outer_core,
            outer_chip,
            outer_diag,
        )
        parts += [kept, to_chip(back)]
    return block_call(functools.partial(join_kernel, sizes), [perturbation.shape])(own, *parts)[0]


def solution(mesh):
    placed = (
        P("harm", None, None, ("parts", "tile"), None),
        P("harm", None, None, ("parts", "tile"), None),
        P(("parts", "tile"), None),
    )

    def chosen(perturbation, base_flow, viscosity):
        two_chips = mesh.shape["harm"] == 2 * 2
        whole_tiles = perturbation.shape[3] % 16 == 0 and perturbation.shape[4] % 128 == 0
        body = paired_shards if two_chips and whole_tiles else shards
        return body(perturbation, base_flow, viscosity)

    return jax.shard_map(
        chosen,
        mesh=mesh,
        in_specs=placed,
        out_specs=P("harm", None, None, ("parts", "tile"), None),
        check_vma=False,
    )
```

```python
import functools

import jax
import jax.numpy as jnp
import numpy as np
from jax import lax
from jax.experimental import pallas as pl
from jax.experimental.pallas import tpu as pltpu
from jax.sharding import PartitionSpec as P

omega_base = 0.25


def extended(cells, sides, width):
    for axis, dim in sides:
        count = lax.axis_size(axis)
        head = lax.slice_in_dim(cells, 0, width, axis=dim)
        tail = lax.slice_in_dim(cells, cells.shape[dim] - width, cells.shape[dim], axis=dim)
        cells = jnp.concatenate(
            [
                lax.ppermute(tail, axis, [(i, (i + 1) % count) for i in range(count)]),
                cells,
                lax.ppermute(head, axis, [((i + 1) % count, i) for i in range(count)]),
            ],
            axis=dim,
        )
    return cells


def shifted(value, axis, steps):
    count = lax.axis_size(axis)
    pairs = [(source, (source + steps) % count) for source in range(count)]
    return lax.ppermute(value, axis, pairs)


def split_rows(padded):
    middle = padded[..., 1:-1, :]
    grad_x = 0.5 * (padded[..., 2:, :] - padded[..., :-2, :])
    grad_y = 0.5 * (jnp.roll(middle, -1, -1) - jnp.roll(middle, 1, -1))
    return (middle, grad_x, grad_y)


def diffusion(padded, visc_padded):
    middle = padded[..., 1:-1, :]
    center = visc_padded[1:-1]
    east_face = 0.5 * (center + visc_padded[2:])
    west_face = 0.5 * (center + visc_padded[:-2])
    north_face = 0.5 * (center + jnp.roll(center, -1, -1))
    south_face = 0.5 * (center + jnp.roll(center, 1, -1))
    return (
        east_face * (padded[..., 2:, :] - middle)
        - west_face * (middle - padded[..., :-2, :])
        + north_face * (jnp.roll(middle, -1, -1) - middle)
        - south_face * (middle - jnp.roll(middle, 1, -1))
    )


def acoustic(grad_x, grad_y):
    dilation = grad_x[..., 1, :, :] + grad_y[..., 2, :, :]
    return jnp.stack(
        [dilation, grad_x[..., 4, :, :], grad_y[..., 4, :, :], jnp.zeros_like(dilation), dilation],
        axis=-3,
    )


def own_terms(middle, grad_x, grad_y, damping, frequency):
    rotation = jnp.stack([-frequency * middle[:, 1], frequency * middle[:, 0]], axis=1)
    return rotation + acoustic(grad_x, grad_y) - damping


def coupling(
    u_real, u_imag, v_real, v_imag, g_real, g_imag, q_real, q_imag, x_real, x_imag, y_real, y_imag
):
    real_part = (
        u_real * x_real
        - u_imag * x_imag
        + v_real * y_real
        - v_imag * y_imag
        + g_real * q_real
        - g_imag * q_imag
    )
    imag_part = (
        u_real * x_imag
        + u_imag * x_real
        + v_real * y_imag
        + v_imag * y_real
        + g_real * q_imag
        + g_imag * q_real
    )
    return (real_part, imag_part)


def block_terms(blocks, middle, grad_x, grad_y):
    local_count = middle.shape[0]
    index_table = np.array(
        [
            [local_count + target - source for source in range(local_count)]
            for target in range(local_count)
        ],
        dtype=np.int32,
    )
    chosen = blocks[index_table]

    def base_part(complex_index, field_index):
        return chosen[:, :, complex_index, field_index][:, :, None]

    def moved_part(values, complex_index):
        return values[None, :, complex_index]

    real_part, imag_part = coupling(
        base_part(0, 0),
        base_part(1, 0),
        base_part(0, 1),
        base_part(1, 1),
        base_part(0, 2),
        base_part(1, 2),
        moved_part(middle, 0),
        moved_part(middle, 1),
        moved_part(grad_x, 0),
        moved_part(grad_x, 1),
        moved_part(grad_y, 0),
        moved_part(grad_y, 1),
    )
    return jnp.stack([jnp.sum(real_part, axis=1), jnp.sum(imag_part, axis=1)], axis=1)


def shards(perturbation, base_flow, viscosity):
    local_count = perturbation.shape[0]
    width_x = perturbation.shape[3]
    width_y = perturbation.shape[4]
    groups = lax.axis_size("harm")
    first_index = lax.axis_index("harm") * local_count
    flattened = perturbation.reshape(local_count * 10, width_x, width_y)
    stacked = jnp.concatenate([flattened, viscosity[None]], axis=0)
    padded = extended(stacked, (("tile", 1),), 1)
    own_padded = padded[:-1].reshape(local_count, 2, 5, width_x + 2, width_y)
    visc_padded = padded[-1]
    numbers = first_index + jnp.arange(local_count, dtype=jnp.int32)
    total_count = local_count * groups
    signed = jnp.where(numbers < total_count // 2, numbers, numbers - total_count)
    frequency = (omega_base * signed.astype(jnp.float32)).reshape(local_count, 1, 1, 1)
    middle, grad_x, grad_y = split_rows(own_padded)
    summed = own_terms(middle, grad_x, grad_y, diffusion(own_padded, visc_padded), frequency)
    whole_base = lax.all_gather(base_flow, "harm", axis=0, tiled=True)

    def base_pair(position, earlier):
        before = lax.dynamic_slice_in_dim(
            whole_base, (position + groups - 1) % groups * local_count, local_count, 0
        )
        current = lax.dynamic_slice_in_dim(whole_base, position * local_count, local_count, 0)
        return (jnp.concatenate([before, current], axis=0), earlier)

    earlier = base_flow
    moving = own_padded

    def advance(moving):
        moved = shifted(moving, "harm", 1)
        return (moved, moved)

    blocks, earlier = base_pair(0, earlier)
    summed = summed + block_terms(blocks, middle, grad_x, grad_y)

    def advance_step(position, carried):
        summed, moving, earlier = carried
        moving, rimmed = advance(moving)
        blocks, earlier = base_pair(position, earlier)
        values, slope_x, slope_y = split_rows(rimmed)
        return (summed + block_terms(blocks, values, slope_x, slope_y), moving, earlier)

    summed, moving, earlier = lax.fori_loop(1, groups, advance_step, (summed, moving, earlier))
    return summed


def ceil_to(count, unit):
    return -(-count // unit) * unit


scoped_bytes = 12 * 1024 * 1024
in_vmem = pl.BlockSpec(memory_space=pltpu.VMEM)
anywhere = pl.BlockSpec(memory_space=pl.ANY)


def lanes_next(value):
    return pltpu.roll(value, value.shape[1] - 1, 1)


def lanes_before(value):
    return pltpu.roll(value, 1, 1)


def rows_next(value, below):
    count = value.shape[0]
    row = lax.broadcasted_iota(jnp.int32, value.shape, 0)
    return jnp.where(row == count - 1, below, pltpu.roll(value, count - 1, 0))


def rows_before(value, above):
    row = lax.broadcasted_iota(jnp.int32, value.shape, 0)
    return jnp.where(row == 0, above, pltpu.roll(value, 1, 0))


class Sizes:
    def __init__(self, perturbation, groups):
        self.local, _, self.fields, self.width, self.columns = perturbation.shape
        self.groups = groups
        self.total = self.local * groups
        self.components = self.local * 2 * self.fields
        self.edge = ceil_to(self.components + 1, 8)
        cut = self.fields - 1
        self.chunks = ((0, cut), (cut, self.fields))

    def at(self, harmonic, part, field):
        return (harmonic * 2 + part) * self.fields + field

    def chunk_shape(self, chunk, harmonics):
        first, last = self.chunks[chunk]
        return (harmonics, 2, last - first, self.width, self.columns)

    def each(self):
        for harmonic in range(self.local):
            for part in range(2):
                for field in range(self.fields):
                    yield harmonic, part, field


def pack_kernel(sizes, q_ref, visc_ref, first_ref, second_ref, up_ref, down_ref):
    last = sizes.width - 1
    for harmonic, part, field in sizes.each():
        at = sizes.at(harmonic, part, field)
        up_ref[at : at + 1, :] = q_ref[harmonic, part, field, last : last + 1, :]
        down_ref[at : at + 1, :] = q_ref[harmonic, part, field, 0:1, :]
    at = sizes.components
    up_ref[at : at + 1, :] = visc_ref[last : last + 1, :]
    down_ref[at : at + 1, :] = visc_ref[0:1, :]
    spare = jnp.zeros((sizes.edge - at - 1, sizes.columns), jnp.float32)
    up_ref[at + 1 :, :] = spare
    down_ref[at + 1 :, :] = spare
    for ref, (begin, end) in zip((first_ref, second_ref), sizes.chunks, strict=True):
        ref[...] = q_ref[:, :, begin:end]


def halo(sizes, ref, at):
    below = sizes.edge + at
    return ref[at : at + 1, :], ref[below : below + 1, :]


def own_terms_of(sizes, chunk, me, q_ref, visc_ref, halo_ref):
    center = visc_ref[...]
    above, below = halo(sizes, halo_ref, sizes.components)
    east = 0.5 * (center + rows_next(center, below))
    west = 0.5 * (center + rows_before(center, above))
    north = 0.5 * (center + lanes_next(center))
    south = 0.5 * (center + lanes_before(center))
    first, last = sizes.chunks[chunk]
    results = {}
    for harmonic in range(sizes.local):
        number = me * sizes.local + harmonic
        signed = jnp.where(number < sizes.total // 2, number, number - sizes.total)
        frequency = omega_base * signed.astype(jnp.float32)
        for part in range(2):

            def beside(field):
                value = q_ref[harmonic, part, field]
                above, below = halo(sizes, halo_ref, sizes.at(harmonic, part, field))
                return value, rows_next(value, below), rows_before(value, above)

            def slope_x(field):
                _, x_next, x_before = beside(field)
                return 0.5 * (x_next - x_before)

            def slope_y(field):
                value = q_ref[harmonic, part, field]
                return 0.5 * (lanes_next(value) - lanes_before(value))

            for field in range(first, last):
                value, x_next, x_before = beside(field)
                damping = (
                    east * (x_next - value)
                    - west * (value - x_before)
                    + north * (lanes_next(value) - value)
                    - south * (value - lanes_before(value))
                )
                turned = q_ref[harmonic, 1 - part, field]
                turn = -frequency if part == 0 else frequency
                term = turn * turned - damping
                if field in (0, 4):
                    term = term + (slope_x(1) + slope_y(2))
                elif field == 1:
                    term = term + slope_x(4)
                elif field == 2:
                    term = term + slope_y(4)
                results[harmonic, part, field] = term
    return results


def couple_kernel(sizes, chunk, *refs):
    base_refs, q_refs, halo_refs, visc_ref = refs[0:4], refs[4:8], refs[8:12], refs[12]
    out_ref, base, values, slopes_x, slopes_y, result, sem = refs[-7:]
    me = lax.axis_index("harm")
    total = sizes.total
    first, last = sizes.chunks[chunk]
    for place in range(4):
        group = lax.bitwise_xor(me, place)
        skipped = first if place < 2 else 0
        for harmonic in range(sizes.local):
            number = group * sizes.local + harmonic
            base[number] = base_refs[place][harmonic]
            for part in range(2):
                for field in range(last - first):
                    value = q_refs[place][harmonic, part, field + skipped]
                    at = sizes.at(harmonic, part, field + first)
                    above, below = halo(sizes, halo_refs[place], at)
                    values[number, part, field] = value
                    slopes_x[number, part, field] = 0.5 * (
                        rows_next(value, below) - rows_before(value, above)
                    )
                    slopes_y[number, part, field] = 0.5 * (lanes_next(value) - lanes_before(value))
    for (harmonic, part, field), term in own_terms_of(
        sizes, chunk, me, q_refs[0], visc_ref, halo_refs[0]
    ).items():
        result[harmonic, part, field - first] = term
    moved_refs = (slopes_x, slopes_y, values)
    for field in range(last - first):
        for start in range(0, sizes.width, 8):
            rows = slice(start, start + 8)
            sums = [
                [result[harmonic, part, field, rows, :] for part in (0, 1)]
                for harmonic in range(sizes.local)
            ]
            for source in range(total):
                moved = [[ref[source, part, field, rows, :] for part in (0, 1)] for ref in moved_refs]
                for harmonic in range(sizes.local):
                    number = me * sizes.local + harmonic
                    at = lax.rem(number - source + total, total)
                    real, imag = sums[harmonic]
                    for term, (m_real, m_imag) in enumerate(moved):
                        c_real = base[at, 0, term, rows, :]
                        c_imag = base[at, 1, term, rows, :]
                        real = real + c_real * m_real - c_imag * m_imag
                        imag = imag + c_real * m_imag + c_imag * m_real
                    sums[harmonic] = [real, imag]
            for harmonic in range(sizes.local):
                for part in (0, 1):
                    result[harmonic, part, field, rows, :] = sums[harmonic][part]
    copy = pltpu.make_async_copy(result, out_ref.at[:, :, first:last], sem)
    copy.start()
    copy.wait()


def paired_shards(perturbation, base_flow, viscosity):
    groups, tiles = lax.axis_size("harm"), lax.axis_size("tile")
    sizes = Sizes(perturbation, groups)

    def to_chip(value):
        return lax.ppermute(value, "harm", [(i, i ^ 2) for i in range(groups)])

    def to_core(value):
        return lax.ppermute(value, "harm", [(i, i ^ 1) for i in range(groups)])

    def along_tile(value, step):
        return lax.ppermute(value, "tile", [(i, (i + step) % tiles) for i in range(tiles)])

    base_chip = to_chip(base_flow)
    edges = jax.ShapeDtypeStruct((sizes.edge, sizes.columns), jnp.float32)
    chunk_types = [
        jax.ShapeDtypeStruct(sizes.chunk_shape(chunk, sizes.local), jnp.float32) for chunk in (0, 1)
    ]
    first, second, up, down = pl.pallas_call(
        functools.partial(pack_kernel, sizes),
        in_specs=[in_vmem] * 2,
        out_shape=[*chunk_types, edges, edges],
        out_specs=[in_vmem] * 4,
        compiler_params=pltpu.CompilerParams(vmem_limit_bytes=scoped_bytes),
    )(perturbation, viscosity)
    base_core = to_core(base_flow)
    q_core = to_core(perturbation)
    above = along_tile(up, 1)
    first_chip = to_chip(first)
    below = along_tile(down, -1)
    halo_own = jnp.concatenate([above, below], axis=0)
    halo_chip = to_chip(halo_own)
    second_chip = to_chip(second)
    halo_core = to_core(halo_own)
    base_diag = to_core(base_chip)
    halo_diag = to_core(halo_chip)
    first_diag = to_core(first_chip)
    second_diag = to_core(second_chip)

    def couple(chunk, chip, diag, earlier):
        moved = pltpu.VMEM(sizes.chunk_shape(chunk, sizes.total), jnp.float32)
        operands = [base_flow, base_core, base_chip, base_diag, perturbation, q_core, chip, diag]
        operands += [halo_own, halo_core, halo_chip, halo_diag, viscosity, *earlier]
        return pl.pallas_call(
            functools.partial(couple_kernel, sizes, chunk),
            in_specs=[in_vmem] * 13 + [anywhere] * len(earlier),
            out_shape=jax.ShapeDtypeStruct(perturbation.shape, jnp.float32),
            out_specs=anywhere,
            input_output_aliases={13: 0} if earlier else {},
            scratch_shapes=[
                pltpu.VMEM((sizes.total, *base_flow.shape[1:]), jnp.float32),
                moved,
                moved,
                moved,
                pltpu.VMEM(sizes.chunk_shape(chunk, sizes.local), jnp.float32),
                pltpu.SemaphoreType.DMA,
            ],
            compiler_params=pltpu.CompilerParams(vmem_limit_bytes=scoped_bytes),
        )(*operands)

    partial = couple(0, first_chip, first_diag, [])
    return couple(1, second_chip, second_diag, [partial])


def solution(mesh):
    placed = (
        P("harm", None, None, ("parts", "tile"), None),
        P("harm", None, None, ("parts", "tile"), None),
        P(("parts", "tile"), None),
    )

    def chosen(perturbation, base_flow, viscosity):
        two_chips = mesh.shape["harm"] == 2 * 2
        whole_tiles = perturbation.shape[3] % 8 == 0 and perturbation.shape[4] % 128 == 0
        body = paired_shards if two_chips and whole_tiles else shards
        return body(perturbation, base_flow, viscosity)

    return jax.shard_map(
        chosen,
        mesh=mesh,
        in_specs=placed,
        out_specs=P("harm", None, None, ("parts", "tile"), None),
        check_vma=False,
    )
```

```python
import functools

import jax
import jax.numpy as jnp
import numpy as np
from jax import lax
from jax.experimental import pallas as pl
from jax.experimental.pallas import tpu as pltpu
from jax.sharding import PartitionSpec as P

omega_base = 0.25


def extended(cells, sides, width):
    for axis, dim in sides:
        count = lax.axis_size(axis)
        head = lax.slice_in_dim(cells, 0, width, axis=dim)
        tail = lax.slice_in_dim(cells, cells.shape[dim] - width, cells.shape[dim], axis=dim)
        cells = jnp.concatenate(
            [
                lax.ppermute(tail, axis, [(i, (i + 1) % count) for i in range(count)]),
                cells,
                lax.ppermute(head, axis, [((i + 1) % count, i) for i in range(count)]),
            ],
            axis=dim,
        )
    return cells


def shifted(value, axis, steps):
    count = lax.axis_size(axis)
    pairs = [(source, (source + steps) % count) for source in range(count)]
    return lax.ppermute(value, axis, pairs)


def split_rows(padded):
    middle = padded[..., 1:-1, :]
    grad_x = 0.5 * (padded[..., 2:, :] - padded[..., :-2, :])
    grad_y = 0.5 * (jnp.roll(middle, -1, -1) - jnp.roll(middle, 1, -1))
    return (middle, grad_x, grad_y)


def diffusion(padded, visc_padded):
    middle = padded[..., 1:-1, :]
    center = visc_padded[1:-1]
    east_face = 0.5 * (center + visc_padded[2:])
    west_face = 0.5 * (center + visc_padded[:-2])
    north_face = 0.5 * (center + jnp.roll(center, -1, -1))
    south_face = 0.5 * (center + jnp.roll(center, 1, -1))
    return (
        east_face * (padded[..., 2:, :] - middle)
        - west_face * (middle - padded[..., :-2, :])
        + north_face * (jnp.roll(middle, -1, -1) - middle)
        - south_face * (middle - jnp.roll(middle, 1, -1))
    )


def acoustic(grad_x, grad_y):
    dilation = grad_x[..., 1, :, :] + grad_y[..., 2, :, :]
    return jnp.stack(
        [dilation, grad_x[..., 4, :, :], grad_y[..., 4, :, :], jnp.zeros_like(dilation), dilation],
        axis=-3,
    )


def own_terms(middle, grad_x, grad_y, damping, frequency):
    rotation = jnp.stack([-frequency * middle[:, 1], frequency * middle[:, 0]], axis=1)
    return rotation + acoustic(grad_x, grad_y) - damping


def coupling(
    u_real, u_imag, v_real, v_imag, g_real, g_imag, q_real, q_imag, x_real, x_imag, y_real, y_imag
):
    real_part = (
        u_real * x_real
        - u_imag * x_imag
        + v_real * y_real
        - v_imag * y_imag
        + g_real * q_real
        - g_imag * q_imag
    )
    imag_part = (
        u_real * x_imag
        + u_imag * x_real
        + v_real * y_imag
        + v_imag * y_real
        + g_real * q_imag
        + g_imag * q_real
    )
    return (real_part, imag_part)


def block_terms(blocks, middle, grad_x, grad_y):
    local_count = middle.shape[0]
    index_table = np.array(
        [
            [local_count + target - source for source in range(local_count)]
            for target in range(local_count)
        ],
        dtype=np.int32,
    )
    chosen = blocks[index_table]

    def base_part(complex_index, field_index):
        return chosen[:, :, complex_index, field_index][:, :, None]

    def moved_part(values, complex_index):
        return values[None, :, complex_index]

    real_part, imag_part = coupling(
        base_part(0, 0),
        base_part(1, 0),
        base_part(0, 1),
        base_part(1, 1),
        base_part(0, 2),
        base_part(1, 2),
        moved_part(middle, 0),
        moved_part(middle, 1),
        moved_part(grad_x, 0),
        moved_part(grad_x, 1),
        moved_part(grad_y, 0),
        moved_part(grad_y, 1),
    )
    return jnp.stack([jnp.sum(real_part, axis=1), jnp.sum(imag_part, axis=1)], axis=1)


def shards(perturbation, base_flow, viscosity):
    local_count = perturbation.shape[0]
    width_x = perturbation.shape[3]
    width_y = perturbation.shape[4]
    groups = lax.axis_size("harm")
    first_index = lax.axis_index("harm") * local_count
    flattened = perturbation.reshape(local_count * 10, width_x, width_y)
    stacked = jnp.concatenate([flattened, viscosity[None]], axis=0)
    padded = extended(stacked, (("tile", 1),), 1)
    own_padded = padded[:-1].reshape(local_count, 2, 5, width_x + 2, width_y)
    visc_padded = padded[-1]
    numbers = first_index + jnp.arange(local_count, dtype=jnp.int32)
    total_count = local_count * groups
    signed = jnp.where(numbers < total_count // 2, numbers, numbers - total_count)
    frequency = (omega_base * signed.astype(jnp.float32)).reshape(local_count, 1, 1, 1)
    middle, grad_x, grad_y = split_rows(own_padded)
    summed = own_terms(middle, grad_x, grad_y, diffusion(own_padded, visc_padded), frequency)
    whole_base = lax.all_gather(base_flow, "harm", axis=0, tiled=True)

    def base_pair(position, earlier):
        before = lax.dynamic_slice_in_dim(
            whole_base, (position + groups - 1) % groups * local_count, local_count, 0
        )
        current = lax.dynamic_slice_in_dim(whole_base, position * local_count, local_count, 0)
        return (jnp.concatenate([before, current], axis=0), earlier)

    earlier = base_flow
    moving = own_padded

    def advance(moving):
        moved = shifted(moving, "harm", 1)
        return (moved, moved)

    blocks, earlier = base_pair(0, earlier)
    summed = summed + block_terms(blocks, middle, grad_x, grad_y)

    def advance_step(position, carried):
        summed, moving, earlier = carried
        moving, rimmed = advance(moving)
        blocks, earlier = base_pair(position, earlier)
        values, slope_x, slope_y = split_rows(rimmed)
        return (summed + block_terms(blocks, values, slope_x, slope_y), moving, earlier)

    summed, moving, earlier = lax.fori_loop(1, groups, advance_step, (summed, moving, earlier))
    return summed


def ceil_to(count, unit):
    return -(-count // unit) * unit


scoped_bytes = 12 * 1024 * 1024
in_vmem = pl.BlockSpec(memory_space=pltpu.VMEM)
anywhere = pl.BlockSpec(memory_space=pl.ANY)


def lanes_next(value):
    return pltpu.roll(value, value.shape[1] - 1, 1)


def lanes_before(value):
    return pltpu.roll(value, 1, 1)


def rows_next(value, below):
    count = value.shape[0]
    row = lax.broadcasted_iota(jnp.int32, value.shape, 0)
    return jnp.where(row == count - 1, below, pltpu.roll(value, count - 1, 0))


def rows_before(value, above):
    row = lax.broadcasted_iota(jnp.int32, value.shape, 0)
    return jnp.where(row == 0, above, pltpu.roll(value, 1, 0))


class Sizes:
    def __init__(self, perturbation, groups):
        self.local, _, self.fields, self.width, self.columns = perturbation.shape
        self.groups = groups
        self.total = self.local * groups
        self.components = self.local * 2 * self.fields
        self.edge = ceil_to(self.components + 1, 8)
        cut = self.fields - 1
        self.moved, self.sent = (0, cut), (cut, self.fields)
        self.block_rows = self.local * 2 * (self.fields - cut) * self.width
        self.message_rows = ceil_to(self.block_rows + self.local * 2 * cut * 2, 8)

    def at(self, harmonic, part, field):
        return (harmonic * 2 + part) * self.fields + field

    def block(self, harmonic, part, field):
        first, last = self.sent
        start = ((harmonic * 2 + part) * (last - first) + field - first) * self.width
        return slice(start, start + self.width)

    def rim(self, harmonic, part, field, side):
        first, last = self.moved
        at = ((harmonic * 2 + part) * (last - first) + field - first) * 2 + side
        return slice(self.block_rows + at, self.block_rows + at + 1)

    def shape(self, harmonics, fields):
        return (harmonics, 2, fields[1] - fields[0], self.width, self.columns)

    def each(self):
        for harmonic in range(self.local):
            for part in range(2):
                for field in range(self.fields):
                    yield harmonic, part, field


def fetch_kernel(sizes, q_from, visc_from, q_ref, visc_ref, moved_ref, q_sem, visc_sem):
    copies = (
        pltpu.make_async_copy(q_from, q_ref, q_sem),
        pltpu.make_async_copy(visc_from, visc_ref, visc_sem),
    )
    for copy in copies:
        copy.start()
    for copy in copies:
        copy.wait()
    moved_ref[...] = q_ref[:, :, sizes.moved[0] : sizes.moved[1]]


def edge_kernel(row):
    def kernel(sizes, q_ref, visc_ref, *refs):
        edge_ref = refs[-1]
        rows = slice(row, row + 1) if row >= 0 else slice(sizes.width - 1, sizes.width)
        for harmonic, part, field in sizes.each():
            at = sizes.at(harmonic, part, field)
            edge_ref[at : at + 1, :] = q_ref[harmonic, part, field, rows, :]
        at = sizes.components
        edge_ref[at : at + 1, :] = visc_ref[rows, :]
        edge_ref[at + 1 :, :] = jnp.zeros((sizes.edge - at - 1, sizes.columns), jnp.float32)

    return kernel


def halo(sizes, ref, at):
    below = sizes.edge + at
    return ref[at : at + 1, :], ref[below : below + 1, :]


def slope_y(value):
    return 0.5 * (lanes_next(value) - lanes_before(value))


def slope_x(value, above, below):
    return 0.5 * (rows_next(value, below) - rows_before(value, above))


def add_products(sums, chosen, moved):
    real, imag = sums
    for (c_real, c_imag), (m_real, m_imag) in zip(chosen, moved, strict=True):
        more_real = c_real * m_real - c_imag * m_imag
        more_imag = c_real * m_imag + c_imag * m_real
        real = more_real if real is None else real + more_real
        imag = more_imag if imag is None else imag + more_imag
    return real, imag


def chosen_rows(sizes, base, target, source, rows):
    at = lax.rem(target - source + sizes.total, sizes.total)
    return [[base[at, part, term, rows, :] for part in (0, 1)] for term in range(3)]


def result_kernel(
    sizes, base_a, base_b, base_c, base_d, q_ref, halo_ref, near_ref, far_ref, base
):
    me = lax.axis_index("harm")
    for place, ref in enumerate((base_a, base_b, base_c, base_d)):
        for harmonic in range(sizes.local):
            base[lax.bitwise_xor(me, place) * sizes.local + harmonic] = ref[harmonic]
    targets = [
        (lax.bitwise_xor(me, place) * sizes.local + harmonic, ref, harmonic)
        for place, ref in ((2, near_ref), (3, far_ref))
        for harmonic in range(sizes.local)
    ]
    first, last = sizes.sent
    parts = (0, 1)
    for field in range(first, last):
        moved = []
        for harmonic in range(sizes.local):
            terms = [[], [], []]
            for part in parts:
                value = q_ref[harmonic, part, field]
                above, below = halo(sizes, halo_ref, sizes.at(harmonic, part, field))
                for term, what in zip(
                    terms, (slope_x(value, above, below), slope_y(value), value), strict=True
                ):
                    term.append(what)
            moved.append(terms)
        for start in range(0, sizes.width, 8):
            rows = slice(start, start + 8)
            for target, ref, harmonic in targets:
                sums = (None, None)
                for source in range(sizes.local):
                    chosen = chosen_rows(sizes, base, target, me * sizes.local + source, rows)
                    cut = [[value[rows] for value in term] for term in moved[source]]
                    sums = add_products(sums, chosen, cut)
                for part in parts:
                    at = sizes.block(harmonic, part, field).start + start
                    ref[at : at + 8, :] = sums[part]
    first, last = sizes.moved
    for side, row, sign in ((0, 0, -0.5), (1, sizes.width - 1, 0.5)):
        outside = [
            [
                jnp.concatenate(
                    [
                        halo(sizes, halo_ref, sizes.at(harmonic, part, field))[side]
                        for field in range(first, last)
                    ],
                    axis=0,
                )
                for part in parts
            ]
            for harmonic in range(sizes.local)
        ]
        for target, ref, harmonic in targets:
            real = imag = 0.0
            for source in range(sizes.local):
                at = lax.rem(target - (me * sizes.local + source) + sizes.total, sizes.total)
                u_real = sign * base[at, 0, 0, row : row + 1, :]
                u_imag = sign * base[at, 1, 0, row : row + 1, :]
                q_real, q_imag = outside[source]
                real = real + u_real * q_real - u_imag * q_imag
                imag = imag + u_real * q_imag + u_imag * q_real
            for part, value in zip(parts, (real, imag), strict=True):
                for field in range(first, last):
                    at = field - first
                    ref[sizes.rim(harmonic, part, field, side), :] = value[at : at + 1, :]
    tail = sizes.block_rows + sizes.local * 2 * (last - first) * 2
    if tail < sizes.message_rows:
        for ref in (near_ref, far_ref):
            ref[tail:, :] = jnp.zeros((sizes.message_rows - tail, sizes.columns), jnp.float32)


def own_terms_into(sizes, q_ref, visc_ref, halo_ref, sum_ref):
    me = lax.axis_index("harm")
    center = visc_ref[...]
    above, below = halo(sizes, halo_ref, sizes.components)
    east = 0.5 * (center + rows_next(center, below))
    west = 0.5 * (center + rows_before(center, above))
    north = 0.5 * (center + lanes_next(center))
    south = 0.5 * (center + lanes_before(center))
    for harmonic in range(sizes.local):
        number = me * sizes.local + harmonic
        signed = jnp.where(number < sizes.total // 2, number, number - sizes.total)
        frequency = omega_base * signed.astype(jnp.float32)
        for part in range(2):
            turn = -frequency if part == 0 else frequency
            terms = {}
            for field in range(sizes.fields):
                value = q_ref[harmonic, part, field]
                above, below = halo(sizes, halo_ref, sizes.at(harmonic, part, field))
                x_next, x_before = rows_next(value, below), rows_before(value, above)
                y_next, y_before = lanes_next(value), lanes_before(value)
                damping = (
                    east * (x_next - value)
                    - west * (value - x_before)
                    + north * (y_next - value)
                    - south * (value - y_before)
                )
                terms[field] = turn * q_ref[harmonic, 1 - part, field] - damping
                if field == 1:
                    dilation = 0.5 * (x_next - x_before)
                elif field == 2:
                    dilation = dilation + 0.5 * (y_next - y_before)
                elif field == 4:
                    terms[1] = terms[1] + 0.5 * (x_next - x_before)
                    terms[2] = terms[2] + 0.5 * (y_next - y_before)
            terms[0] = terms[0] + dilation
            terms[4] = terms[4] + dilation
            for field in range(sizes.fields):
                sum_ref[harmonic, part, field] = terms[field]


def couple(sizes, base, place, fields, start_from, q_ref, halo_ref, slopes, store):
    me = lax.axis_index("harm")
    slopes_x, slopes_y = slopes
    group = lax.bitwise_xor(me, place)
    for field in range(*fields):
        for harmonic in range(sizes.local):
            for part in (0, 1):
                value = q_ref[harmonic, part, field]
                above = below = 0.0
                if halo_ref is not None:
                    above, below = halo(sizes, halo_ref, sizes.at(harmonic, part, field))
                slopes_x[harmonic, part] = slope_x(value, above, below)
                slopes_y[harmonic, part] = slope_y(value)
        for start in range(0, sizes.width, 8):
            rows = slice(start, start + 8)
            sums = [
                [start_from(harmonic, part, field, rows) for part in (0, 1)]
                for harmonic in range(sizes.local)
            ]
            for source in range(sizes.local):
                moved = [
                    [slopes_x[source, part, rows, :] for part in (0, 1)],
                    [slopes_y[source, part, rows, :] for part in (0, 1)],
                    [q_ref[source, part, field, rows, :] for part in (0, 1)],
                ]
                for harmonic in range(sizes.local):
                    target = me * sizes.local + harmonic
                    number = group * sizes.local + source
                    chosen = chosen_rows(sizes, base, target, number, rows)
                    sums[harmonic] = add_products(sums[harmonic], chosen, moved)
            for harmonic in range(sizes.local):
                for part in (0, 1):
                    store(harmonic, part, field, rows, sums[harmonic][part])


def reader(ref):
    return lambda harmonic, part, field, rows: ref[harmonic, part, field, rows, :]


def writer(ref):
    def store(harmonic, part, field, rows, value):
        ref[harmonic, part, field, rows, :] = value

    return store


def own_kernel(sizes, base, q_ref, halo_ref, visc_ref, _, sum_ref, *slopes):
    own_terms_into(sizes, q_ref, visc_ref, halo_ref, sum_ref)
    everything = (0, sizes.fields)
    couple(
        sizes, base, 0, everything, reader(sum_ref), q_ref, halo_ref, slopes, writer(sum_ref)
    )


def core_kernel(sizes, base, q_ref, halo_ref, before_ref, sum_ref, *slopes):
    everything = (0, sizes.fields)
    couple(
        sizes, base, 1, everything, reader(before_ref), q_ref, halo_ref, slopes, writer(sum_ref)
    )


def far_kernel(place):
    def kernel(sizes, base, q_ref, before_ref, sum_ref, *slopes):
        couple(
            sizes, base, place, sizes.moved, reader(before_ref), q_ref, None, slopes,
            writer(sum_ref),
        )

    return kernel


def pass_kernel(sizes, values, after, same):
    pass


def sent_kernel(sizes, near_ref, message, _, sum_ref):
    first = sizes.sent[0]
    for field in range(*sizes.sent):
        for harmonic in range(sizes.local):
            for part in (0, 1):
                more = message[sizes.block(harmonic, part, field), :]
                sum_ref[harmonic, part, field - first] = near_ref[harmonic, part, field] + more


def last_kernel(
    sizes, base, q_diag, sent_ref, far_ref, message, out_ref, slopes_x, slopes_y, result, sems
):
    copies = []

    def send(source, field):
        copies.append(
            pltpu.make_async_copy(source, out_ref.at[:, :, field], sems.at[field])
        )
        copies[-1].start()

    for field in range(*sizes.sent):
        send(sent_ref.at[:, :, field - sizes.sent[0]], field)
    for field in range(*sizes.moved):
        couple(
            sizes, base, 3, (field, field + 1), reader(far_ref), q_diag, None, (slopes_x, slopes_y),
            writer(result),
        )
        for harmonic in range(sizes.local):
            for part in (0, 1):
                for side, row in ((0, 0), (1, sizes.width - 1)):
                    more = message[sizes.rim(harmonic, part, field, side), :]
                    result[harmonic, part, field, row : row + 1, :] += more
        send(result.at[:, :, field], field)
    for copy in copies:
        copy.wait()


def paired_shards(perturbation, base_flow, viscosity):
    groups, tiles = lax.axis_size("harm"), lax.axis_size("tile")
    sizes = Sizes(perturbation, groups)

    def to_chip(value):
        return lax.ppermute(value, "harm", [(i, i ^ 2) for i in range(groups)])

    def to_core(value):
        return lax.ppermute(value, "harm", [(i, i ^ 1) for i in range(groups)])

    def along_tile(value, step):
        return lax.ppermute(value, "tile", [(i, (i + step) % tiles) for i in range(tiles)])

    def array(*shape):
        return jax.ShapeDtypeStruct(shape, jnp.float32)

    def call(
        kernel, operands, outs, scratch=(), in_specs=None, out_specs=None, flops=1, aliases=None
    ):
        return pl.pallas_call(
            functools.partial(kernel, sizes),
            in_specs=in_specs or [in_vmem] * len(operands),
            out_shape=outs,
            out_specs=out_specs or [in_vmem] * len(outs),
            scratch_shapes=scratch,
            input_output_aliases=aliases or {},
            cost_estimate=pl.CostEstimate(flops=flops, bytes_accessed=1, transcendentals=0),
            compiler_params=pltpu.CompilerParams(vmem_limit_bytes=scoped_bytes),
        )(*operands)

    slopes = [pltpu.VMEM((sizes.local, 2, sizes.width, sizes.columns), jnp.float32)] * 2
    edges = array(sizes.edge, sizes.columns)
    message = array(sizes.message_rows, sizes.columns)

    base_chip = to_chip(base_flow)
    held, visc, moved = call(
        fetch_kernel,
        [pltpu.with_memory_space_constraint(x, pltpu.HBM) for x in (perturbation, viscosity)],
        [
            array(*perturbation.shape),
            array(*viscosity.shape),
            array(*sizes.shape(sizes.local, sizes.moved)),
        ],
        [pltpu.SemaphoreType.DMA] * 2,
        [anywhere] * 2,
    )
    up = call(edge_kernel(-1), (held, visc), [edges])[0]
    base_core = to_core(base_flow)
    above = along_tile(up, 1)
    moved_chip = to_chip(moved)
    down = call(
        edge_kernel(0), (held, visc, base_core), [edges], in_specs=[in_vmem] * 2 + [anywhere]
    )[0]
    below = along_tile(down, -1)
    halo_own = jnp.concatenate([above, below], axis=0)
    halo_core = to_core(halo_own)
    base_diag = to_core(base_chip)
    near, far, base = call(
        result_kernel,
        (base_flow, base_core, base_chip, base_diag, held, halo_own),
        [message, message, array(sizes.total, *base_flow.shape[1:])],
    )
    message_out = near + to_core(far)
    results = to_chip(message_out)
    held_core = to_core(lax.optimization_barrier((held, near))[0])
    own_sum = call(
        own_kernel,
        (base, held, halo_own, visc, message_out),
        [array(*perturbation.shape)],
        slopes,
        [in_vmem] * 4 + [anywhere],
    )[0]
    near_sum = call(
        core_kernel, (base, held_core, halo_core, own_sum), [array(*perturbation.shape)], slopes
    )[0]
    moved_here = call(
        pass_kernel,
        (moved_chip, own_sum),
        array(*moved_chip.shape),
        in_specs=[anywhere] * 2,
        out_specs=anywhere,
        flops=10**9,
        aliases={0: 0},
    )
    moved_diag = to_core(moved_here)
    far_sum = call(
        far_kernel(2),
        (base, moved_here, near_sum),
        [array(*sizes.shape(sizes.local, sizes.moved))],
        slopes,
    )[0]
    sent_sum = call(
        sent_kernel,
        (near_sum, results, far_sum),
        [array(*sizes.shape(sizes.local, sizes.sent))],
        flops=2*10**9,
        in_specs=[in_vmem, in_vmem, anywhere],
    )[0]
    return call(
        last_kernel,
        (base, moved_diag, sent_sum, far_sum, results),
        array(*perturbation.shape),
        [
            *slopes,
            pltpu.VMEM(sizes.shape(sizes.local, sizes.moved), jnp.float32),
            pltpu.SemaphoreType.DMA((sizes.fields,)),
        ],
        out_specs=anywhere,
    )


def solution(mesh):
    placed = (
        P("harm", None, None, ("parts", "tile"), None),
        P("harm", None, None, ("parts", "tile"), None),
        P(("parts", "tile"), None),
    )

    def chosen(perturbation, base_flow, viscosity):
        two_chips = mesh.shape["harm"] == 2 * 2
        whole_tiles = perturbation.shape[3] % 8 == 0 and perturbation.shape[4] % 128 == 0
        body = paired_shards if two_chips and whole_tiles else shards
        return body(perturbation, base_flow, viscosity)

    return jax.shard_map(
        chosen,
        mesh=mesh,
        in_specs=placed,
        out_specs=P("harm", None, None, ("parts", "tile"), None),
        check_vma=False,
    )
```

```python
import functools

import jax
import jax.numpy as jnp
import numpy as np
from jax import lax
from jax.experimental import pallas as pl
from jax.experimental.pallas import tpu as pltpu
from jax.sharding import PartitionSpec as P

omega_base = 0.25


def extended(cells, sides, width):
    for axis, dim in sides:
        count = lax.axis_size(axis)
        head = lax.slice_in_dim(cells, 0, width, axis=dim)
        tail = lax.slice_in_dim(cells, cells.shape[dim] - width, cells.shape[dim], axis=dim)
        cells = jnp.concatenate(
            [
                lax.ppermute(tail, axis, [(i, (i + 1) % count) for i in range(count)]),
                cells,
                lax.ppermute(head, axis, [((i + 1) % count, i) for i in range(count)]),
            ],
            axis=dim,
        )
    return cells


def shifted(value, axis, steps):
    count = lax.axis_size(axis)
    pairs = [(source, (source + steps) % count) for source in range(count)]
    return lax.ppermute(value, axis, pairs)


def split_rows(padded):
    middle = padded[..., 1:-1, :]
    grad_x = 0.5 * (padded[..., 2:, :] - padded[..., :-2, :])
    grad_y = 0.5 * (jnp.roll(middle, -1, -1) - jnp.roll(middle, 1, -1))
    return (middle, grad_x, grad_y)


def diffusion(padded, visc_padded):
    middle = padded[..., 1:-1, :]
    center = visc_padded[1:-1]
    east_face = 0.5 * (center + visc_padded[2:])
    west_face = 0.5 * (center + visc_padded[:-2])
    north_face = 0.5 * (center + jnp.roll(center, -1, -1))
    south_face = 0.5 * (center + jnp.roll(center, 1, -1))
    return (
        east_face * (padded[..., 2:, :] - middle)
        - west_face * (middle - padded[..., :-2, :])
        + north_face * (jnp.roll(middle, -1, -1) - middle)
        - south_face * (middle - jnp.roll(middle, 1, -1))
    )


def acoustic(grad_x, grad_y):
    dilation = grad_x[..., 1, :, :] + grad_y[..., 2, :, :]
    return jnp.stack(
        [dilation, grad_x[..., 4, :, :], grad_y[..., 4, :, :], jnp.zeros_like(dilation), dilation],
        axis=-3,
    )


def own_terms(middle, grad_x, grad_y, damping, frequency):
    rotation = jnp.stack([-frequency * middle[:, 1], frequency * middle[:, 0]], axis=1)
    return rotation + acoustic(grad_x, grad_y) - damping


def coupling(
    u_real, u_imag, v_real, v_imag, g_real, g_imag, q_real, q_imag, x_real, x_imag, y_real, y_imag
):
    real_part = (
        u_real * x_real
        - u_imag * x_imag
        + v_real * y_real
        - v_imag * y_imag
        + g_real * q_real
        - g_imag * q_imag
    )
    imag_part = (
        u_real * x_imag
        + u_imag * x_real
        + v_real * y_imag
        + v_imag * y_real
        + g_real * q_imag
        + g_imag * q_real
    )
    return (real_part, imag_part)


def block_terms(blocks, middle, grad_x, grad_y):
    local_count = middle.shape[0]
    index_table = np.array(
        [
            [local_count + target - source for source in range(local_count)]
            for target in range(local_count)
        ],
        dtype=np.int32,
    )
    chosen = blocks[index_table]

    def base_part(complex_index, field_index):
        return chosen[:, :, complex_index, field_index][:, :, None]

    def moved_part(values, complex_index):
        return values[None, :, complex_index]

    real_part, imag_part = coupling(
        base_part(0, 0),
        base_part(1, 0),
        base_part(0, 1),
        base_part(1, 1),
        base_part(0, 2),
        base_part(1, 2),
        moved_part(middle, 0),
        moved_part(middle, 1),
        moved_part(grad_x, 0),
        moved_part(grad_x, 1),
        moved_part(grad_y, 0),
        moved_part(grad_y, 1),
    )
    return jnp.stack([jnp.sum(real_part, axis=1), jnp.sum(imag_part, axis=1)], axis=1)


def shards(perturbation, base_flow, viscosity):
    local_count = perturbation.shape[0]
    width_x = perturbation.shape[3]
    width_y = perturbation.shape[4]
    groups = lax.axis_size("harm")
    first_index = lax.axis_index("harm") * local_count
    flattened = perturbation.reshape(local_count * 10, width_x, width_y)
    stacked = jnp.concatenate([flattened, viscosity[None]], axis=0)
    padded = extended(stacked, (("tile", 1),), 1)
    own_padded = padded[:-1].reshape(local_count, 2, 5, width_x + 2, width_y)
    visc_padded = padded[-1]
    numbers = first_index + jnp.arange(local_count, dtype=jnp.int32)
    total_count = local_count * groups
    signed = jnp.where(numbers < total_count // 2, numbers, numbers - total_count)
    frequency = (omega_base * signed.astype(jnp.float32)).reshape(local_count, 1, 1, 1)
    middle, grad_x, grad_y = split_rows(own_padded)
    summed = own_terms(middle, grad_x, grad_y, diffusion(own_padded, visc_padded), frequency)
    whole_base = lax.all_gather(base_flow, "harm", axis=0, tiled=True)

    def base_pair(position, earlier):
        before = lax.dynamic_slice_in_dim(
            whole_base, (position + groups - 1) % groups * local_count, local_count, 0
        )
        current = lax.dynamic_slice_in_dim(whole_base, position * local_count, local_count, 0)
        return (jnp.concatenate([before, current], axis=0), earlier)

    earlier = base_flow
    moving = own_padded

    def advance(moving):
        moved = shifted(moving, "harm", 1)
        return (moved, moved)

    blocks, earlier = base_pair(0, earlier)
    summed = summed + block_terms(blocks, middle, grad_x, grad_y)

    def advance_step(position, carried):
        summed, moving, earlier = carried
        moving, rimmed = advance(moving)
        blocks, earlier = base_pair(position, earlier)
        values, slope_x, slope_y = split_rows(rimmed)
        return (summed + block_terms(blocks, values, slope_x, slope_y), moving, earlier)

    summed, moving, earlier = lax.fori_loop(1, groups, advance_step, (summed, moving, earlier))
    return summed


def ceil_to(count, unit):
    return -(-count // unit) * unit


scoped_bytes = 12 * 1024 * 1024
in_vmem = pl.BlockSpec(memory_space=pltpu.VMEM)
anywhere = pl.BlockSpec(memory_space=pl.ANY)


def lanes_next(value):
    return pltpu.roll(value, value.shape[1] - 1, 1)


def lanes_before(value):
    return pltpu.roll(value, 1, 1)


def rows_next(value, below):
    count = value.shape[0]
    row = lax.broadcasted_iota(jnp.int32, value.shape, 0)
    return jnp.where(row == count - 1, below, pltpu.roll(value, count - 1, 0))


def rows_before(value, above):
    row = lax.broadcasted_iota(jnp.int32, value.shape, 0)
    return jnp.where(row == 0, above, pltpu.roll(value, 1, 0))


class Sizes:
    def __init__(self, perturbation, groups):
        self.local, _, self.fields, self.width, self.columns = perturbation.shape
        self.groups = groups
        self.total = self.local * groups
        self.components = self.local * 2 * self.fields
        self.edge = ceil_to(self.components + 1, 8)
        cut = self.fields - 1
        self.moved, self.sent = (0, cut), (cut, self.fields)
        self.block_rows = self.local * 2 * (self.fields - cut) * self.width
        self.message_rows = ceil_to(self.block_rows + self.local * 2 * cut * 2, 8)

    def at(self, harmonic, part, field):
        return (harmonic * 2 + part) * self.fields + field

    def block(self, harmonic, part, field):
        first, last = self.sent
        start = ((harmonic * 2 + part) * (last - first) + field - first) * self.width
        return slice(start, start + self.width)

    def rim(self, harmonic, part, field, side):
        first, last = self.moved
        at = ((harmonic * 2 + part) * (last - first) + field - first) * 2 + side
        return slice(self.block_rows + at, self.block_rows + at + 1)

    def shape(self, harmonics, fields):
        return (harmonics, 2, fields[1] - fields[0], self.width, self.columns)

    def each(self):
        for harmonic in range(self.local):
            for part in range(2):
                for field in range(self.fields):
                    yield harmonic, part, field


def fetch_kernel(sizes, q_from, visc_from, q_ref, visc_ref, moved_ref, q_sem, visc_sem):
    copies = (
        pltpu.make_async_copy(q_from, q_ref, q_sem),
        pltpu.make_async_copy(visc_from, visc_ref, visc_sem),
    )
    for copy in copies:
        copy.start()
    for copy in copies:
        copy.wait()
    moved_ref[...] = q_ref[:, :, sizes.moved[0] : sizes.moved[1]]


def edge_kernel(row):
    def kernel(sizes, q_ref, visc_ref, *refs):
        edge_ref = refs[-1]
        rows = slice(row, row + 1) if row >= 0 else slice(sizes.width - 1, sizes.width)
        for harmonic, part, field in sizes.each():
            at = sizes.at(harmonic, part, field)
            edge_ref[at : at + 1, :] = q_ref[harmonic, part, field, rows, :]
        at = sizes.components
        edge_ref[at : at + 1, :] = visc_ref[rows, :]
        edge_ref[at + 1 :, :] = jnp.zeros((sizes.edge - at - 1, sizes.columns), jnp.float32)

    return kernel


def halo(sizes, ref, at):
    below = sizes.edge + at
    return ref[at : at + 1, :], ref[below : below + 1, :]


def slope_y(value):
    return 0.5 * (lanes_next(value) - lanes_before(value))


def slope_x(value, above, below):
    return 0.5 * (rows_next(value, below) - rows_before(value, above))


def add_products(sums, chosen, moved):
    real, imag = sums
    for (c_real, c_imag), (m_real, m_imag) in zip(chosen, moved, strict=True):
        more_real = c_real * m_real - c_imag * m_imag
        more_imag = c_real * m_imag + c_imag * m_real
        real = more_real if real is None else real + more_real
        imag = more_imag if imag is None else imag + more_imag
    return real, imag


def chosen_rows(sizes, base, target, source, rows):
    at = lax.rem(target - source + sizes.total, sizes.total)
    return [[base[at, part, term, rows, :] for part in (0, 1)] for term in range(3)]


def result_kernel(
    sizes, base_a, base_b, base_c, base_d, q_own, q_core, halo_own, halo_core, out_ref, base
):
    me = lax.axis_index("harm")
    for place, ref in enumerate((base_a, base_b, base_c, base_d)):
        for harmonic in range(sizes.local):
            base[lax.bitwise_xor(me, place) * sizes.local + harmonic] = ref[harmonic]
    targets = [lax.bitwise_xor(me, 2) * sizes.local + harmonic for harmonic in range(sizes.local)]
    sources = [
        (lax.bitwise_xor(me, place) * sizes.local + harmonic, q_ref, halo_ref, harmonic)
        for place, q_ref, halo_ref in ((0, q_own, halo_own), (1, q_core, halo_core))
        for harmonic in range(sizes.local)
    ]
    first, last = sizes.sent
    parts = (0, 1)
    for field in range(first, last):
        moved = []
        for _, q_ref, halo_ref, harmonic in sources:
            terms = [[], [], []]
            for part in parts:
                value = q_ref[harmonic, part, field]
                above, below = halo(sizes, halo_ref, sizes.at(harmonic, part, field))
                for term, what in zip(
                    terms, (slope_x(value, above, below), slope_y(value), value), strict=True
                ):
                    term.append(what)
            moved.append(terms)
        for start in range(0, sizes.width, 8):
            rows = slice(start, start + 8)
            for harmonic, target in enumerate(targets):
                sums = (None, None)
                for terms, (source, _, _, _) in zip(moved, sources, strict=True):
                    chosen = chosen_rows(sizes, base, target, source, rows)
                    cut = [[value[rows] for value in term] for term in terms]
                    sums = add_products(sums, chosen, cut)
                for part in parts:
                    at = sizes.block(harmonic, part, field).start + start
                    out_ref[at : at + 8, :] = sums[part]
    first, last = sizes.moved
    for side, row, sign in ((0, 0, -0.5), (1, sizes.width - 1, 0.5)):
        outside = [
            [
                jnp.concatenate(
                    [
                        halo(sizes, halo_ref, sizes.at(harmonic, part, field))[side]
                        for field in range(first, last)
                    ],
                    axis=0,
                )
                for part in parts
            ]
            for _, _, halo_ref, harmonic in sources
        ]
        for harmonic, target in enumerate(targets):
            real = imag = 0.0
            for (q_real, q_imag), (source, _, _, _) in zip(outside, sources, strict=True):
                at = lax.rem(target - source + sizes.total, sizes.total)
                u_real = sign * base[at, 0, 0, row : row + 1, :]
                u_imag = sign * base[at, 1, 0, row : row + 1, :]
                real = real + u_real * q_real - u_imag * q_imag
                imag = imag + u_real * q_imag + u_imag * q_real
            for part, value in zip(parts, (real, imag), strict=True):
                for field in range(first, last):
                    at = field - first
                    out_ref[sizes.rim(harmonic, part, field, side), :] = value[at : at + 1, :]
    tail = sizes.block_rows + sizes.local * 2 * (last - first) * 2
    if tail < sizes.message_rows:
        out_ref[tail:, :] = jnp.zeros((sizes.message_rows - tail, sizes.columns), jnp.float32)


def own_terms_into(sizes, q_ref, visc_ref, halo_ref, sum_ref):
    me = lax.axis_index("harm")
    center = visc_ref[...]
    above, below = halo(sizes, halo_ref, sizes.components)
    east = 0.5 * (center + rows_next(center, below))
    west = 0.5 * (center + rows_before(center, above))
    north = 0.5 * (center + lanes_next(center))
    south = 0.5 * (center + lanes_before(center))
    for harmonic in range(sizes.local):
        number = me * sizes.local + harmonic
        signed = jnp.where(number < sizes.total // 2, number, number - sizes.total)
        frequency = omega_base * signed.astype(jnp.float32)
        for part in range(2):
            turn = -frequency if part == 0 else frequency
            terms = {}
            for field in range(sizes.fields):
                value = q_ref[harmonic, part, field]
                above, below = halo(sizes, halo_ref, sizes.at(harmonic, part, field))
                x_next, x_before = rows_next(value, below), rows_before(value, above)
                y_next, y_before = lanes_next(value), lanes_before(value)
                damping = (
                    east * (x_next - value)
                    - west * (value - x_before)
                    + north * (y_next - value)
                    - south * (value - y_before)
                )
                terms[field] = turn * q_ref[harmonic, 1 - part, field] - damping
                if field == 1:
                    dilation = 0.5 * (x_next - x_before)
                elif field == 2:
                    dilation = dilation + 0.5 * (y_next - y_before)
                elif field == 4:
                    terms[1] = terms[1] + 0.5 * (x_next - x_before)
                    terms[2] = terms[2] + 0.5 * (y_next - y_before)
            terms[0] = terms[0] + dilation
            terms[4] = terms[4] + dilation
            for field in range(sizes.fields):
                sum_ref[harmonic, part, field] = terms[field]


def couple(sizes, base, place, fields, start_from, q_ref, halo_ref, slopes, store):
    me = lax.axis_index("harm")
    slopes_x, slopes_y = slopes
    group = lax.bitwise_xor(me, place)
    for field in range(*fields):
        for harmonic in range(sizes.local):
            for part in (0, 1):
                value = q_ref[harmonic, part, field]
                above = below = 0.0
                if halo_ref is not None:
                    above, below = halo(sizes, halo_ref, sizes.at(harmonic, part, field))
                slopes_x[harmonic, part] = slope_x(value, above, below)
                slopes_y[harmonic, part] = slope_y(value)
        for start in range(0, sizes.width, 8):
            rows = slice(start, start + 8)
            sums = [
                [start_from(harmonic, part, field, rows) for part in (0, 1)]
                for harmonic in range(sizes.local)
            ]
            for source in range(sizes.local):
                moved = [
                    [slopes_x[source, part, rows, :] for part in (0, 1)],
                    [slopes_y[source, part, rows, :] for part in (0, 1)],
                    [q_ref[source, part, field, rows, :] for part in (0, 1)],
                ]
                for harmonic in range(sizes.local):
                    target = me * sizes.local + harmonic
                    number = group * sizes.local + source
                    chosen = chosen_rows(sizes, base, target, number, rows)
                    sums[harmonic] = add_products(sums[harmonic], chosen, moved)
            for harmonic in range(sizes.local):
                for part in (0, 1):
                    store(harmonic, part, field, rows, sums[harmonic][part])


def reader(ref):
    return lambda harmonic, part, field, rows: ref[harmonic, part, field, rows, :]


def writer(ref):
    def store(harmonic, part, field, rows, value):
        ref[harmonic, part, field, rows, :] = value

    return store


def own_kernel(sizes, base, q_ref, halo_ref, visc_ref, sum_ref, *slopes):
    own_terms_into(sizes, q_ref, visc_ref, halo_ref, sum_ref)
    everything = (0, sizes.fields)
    couple(
        sizes, base, 0, everything, reader(sum_ref), q_ref, halo_ref, slopes, writer(sum_ref)
    )


def core_kernel(sizes, base, q_ref, halo_ref, before_ref, sum_ref, *slopes):
    everything = (0, sizes.fields)
    couple(
        sizes, base, 1, everything, reader(before_ref), q_ref, halo_ref, slopes, writer(sum_ref)
    )


def far_kernel(place):
    def kernel(sizes, base, q_ref, before_ref, sum_ref, *slopes):
        couple(
            sizes, base, place, sizes.moved, reader(before_ref), q_ref, None, slopes,
            writer(sum_ref),
        )

    return kernel


def pass_kernel(sizes, values, after, same):
    pass


def sent_kernel(sizes, near_ref, message, _, sum_ref):
    first = sizes.sent[0]
    for field in range(*sizes.sent):
        for harmonic in range(sizes.local):
            for part in (0, 1):
                more = message[sizes.block(harmonic, part, field), :]
                sum_ref[harmonic, part, field - first] = near_ref[harmonic, part, field] + more


def last_kernel(
    sizes, base, q_diag, sent_ref, far_ref, message, out_ref, slopes_x, slopes_y, result, sems
):
    copies = []

    def send(source, field):
        copies.append(
            pltpu.make_async_copy(source, out_ref.at[:, :, field], sems.at[field])
        )
        copies[-1].start()

    for field in range(*sizes.sent):
        send(sent_ref.at[:, :, field - sizes.sent[0]], field)
    for field in range(*sizes.moved):
        couple(
            sizes, base, 3, (field, field + 1), reader(far_ref), q_diag, None, (slopes_x, slopes_y),
            writer(result),
        )
        for harmonic in range(sizes.local):
            for part in (0, 1):
                for side, row in ((0, 0), (1, sizes.width - 1)):
                    more = message[sizes.rim(harmonic, part, field, side), :]
                    result[harmonic, part, field, row : row + 1, :] += more
        send(result.at[:, :, field], field)
    for copy in copies:
        copy.wait()


def paired_shards(perturbation, base_flow, viscosity):
    groups, tiles = lax.axis_size("harm"), lax.axis_size("tile")
    sizes = Sizes(perturbation, groups)

    def to_chip(value):
        return lax.ppermute(value, "harm", [(i, i ^ 2) for i in range(groups)])

    def to_core(value):
        return lax.ppermute(value, "harm", [(i, i ^ 1) for i in range(groups)])

    def along_tile(value, step):
        return lax.ppermute(value, "tile", [(i, (i + step) % tiles) for i in range(tiles)])

    def array(*shape):
        return jax.ShapeDtypeStruct(shape, jnp.float32)

    def call(
        kernel, operands, outs, scratch=(), in_specs=None, out_specs=None, flops=1, aliases=None
    ):
        return pl.pallas_call(
            functools.partial(kernel, sizes),
            in_specs=in_specs or [in_vmem] * len(operands),
            out_shape=outs,
            out_specs=out_specs or [in_vmem] * len(outs),
            scratch_shapes=scratch,
            input_output_aliases=aliases or {},
            cost_estimate=pl.CostEstimate(flops=flops, bytes_accessed=1, transcendentals=0),
            compiler_params=pltpu.CompilerParams(vmem_limit_bytes=scoped_bytes),
        )(*operands)

    slopes = [pltpu.VMEM((sizes.local, 2, sizes.width, sizes.columns), jnp.float32)] * 2
    edges = array(sizes.edge, sizes.columns)

    base_chip = to_chip(base_flow)
    held, visc, moved = call(
        fetch_kernel,
        [pltpu.with_memory_space_constraint(x, pltpu.HBM) for x in (perturbation, viscosity)],
        [
            array(*perturbation.shape),
            array(*viscosity.shape),
            array(*sizes.shape(sizes.local, sizes.moved)),
        ],
        [pltpu.SemaphoreType.DMA] * 2,
        [anywhere] * 2,
    )
    up = call(edge_kernel(-1), (held, visc), [edges])[0]
    base_core = to_core(base_flow)
    above = along_tile(up, 1)
    moved_chip = to_chip(moved)
    down = call(
        edge_kernel(0), (held, visc, base_core), [edges], in_specs=[in_vmem] * 2 + [anywhere]
    )[0]
    below = along_tile(down, -1)
    halo_own = jnp.concatenate([above, below], axis=0)
    halo_core = to_core(halo_own)
    held_core = to_core(lax.optimization_barrier((held, base_core))[0])
    base_diag = to_core(base_chip)
    message, base = call(
        result_kernel,
        (base_flow, base_core, base_chip, base_diag, held, held_core, halo_own, halo_core),
        [array(sizes.message_rows, sizes.columns), array(sizes.total, *base_flow.shape[1:])],
    )
    results = to_chip(message)
    own_sum = call(
        own_kernel, (base, held, halo_own, visc), [array(*perturbation.shape)], slopes
    )[0]
    near_sum = call(
        core_kernel, (base, held_core, halo_core, own_sum), [array(*perturbation.shape)], slopes
    )[0]
    moved_here = call(
        pass_kernel,
        (moved_chip, own_sum),
        array(*moved_chip.shape),
        in_specs=[anywhere] * 2,
        out_specs=anywhere,
        flops=10**9,
        aliases={0: 0},
    )
    moved_diag = to_core(moved_here)
    far_sum = call(
        far_kernel(2),
        (base, moved_here, near_sum),
        [array(*sizes.shape(sizes.local, sizes.moved))],
        slopes,
    )[0]
    sent_sum = call(
        sent_kernel,
        (near_sum, results, far_sum),
        [array(*sizes.shape(sizes.local, sizes.sent))],
        flops=3*10**9,
        in_specs=[in_vmem, in_vmem, anywhere],
    )[0]
    return call(
        last_kernel,
        (base, moved_diag, sent_sum, far_sum, results),
        array(*perturbation.shape),
        [
            *slopes,
            pltpu.VMEM(sizes.shape(sizes.local, sizes.moved), jnp.float32),
            pltpu.SemaphoreType.DMA((sizes.fields,)),
        ],
        out_specs=anywhere,
    )


def solution(mesh):
    placed = (
        P("harm", None, None, ("parts", "tile"), None),
        P("harm", None, None, ("parts", "tile"), None),
        P(("parts", "tile"), None),
    )

    def chosen(perturbation, base_flow, viscosity):
        two_chips = mesh.shape["harm"] == 2 * 2
        whole_tiles = perturbation.shape[3] % 8 == 0 and perturbation.shape[4] % 128 == 0
        body = paired_shards if two_chips and whole_tiles else shards
        return body(perturbation, base_flow, viscosity)

    return jax.shard_map(
        chosen,
        mesh=mesh,
        in_specs=placed,
        out_specs=P("harm", None, None, ("parts", "tile"), None),
        check_vma=False,
    )
```

```python
import functools

import jax
import jax.numpy as jnp
import numpy as np
from jax import lax
from jax.experimental import pallas as pl
from jax.experimental.pallas import tpu as pltpu
from jax.sharding import PartitionSpec as P

omega_base = 0.25


def extended(cells, sides, width):
    for axis, dim in sides:
        count = lax.axis_size(axis)
        head = lax.slice_in_dim(cells, 0, width, axis=dim)
        tail = lax.slice_in_dim(cells, cells.shape[dim] - width, cells.shape[dim], axis=dim)
        cells = jnp.concatenate(
            [
                lax.ppermute(tail, axis, [(i, (i + 1) % count) for i in range(count)]),
                cells,
                lax.ppermute(head, axis, [((i + 1) % count, i) for i in range(count)]),
            ],
            axis=dim,
        )
    return cells


def shifted(value, axis, steps):
    count = lax.axis_size(axis)
    pairs = [(source, (source + steps) % count) for source in range(count)]
    return lax.ppermute(value, axis, pairs)


def split_rows(padded):
    middle = padded[..., 1:-1, :]
    grad_x = 0.5 * (padded[..., 2:, :] - padded[..., :-2, :])
    grad_y = 0.5 * (jnp.roll(middle, -1, -1) - jnp.roll(middle, 1, -1))
    return (middle, grad_x, grad_y)


def diffusion(padded, visc_padded):
    middle = padded[..., 1:-1, :]
    center = visc_padded[1:-1]
    east_face = 0.5 * (center + visc_padded[2:])
    west_face = 0.5 * (center + visc_padded[:-2])
    north_face = 0.5 * (center + jnp.roll(center, -1, -1))
    south_face = 0.5 * (center + jnp.roll(center, 1, -1))
    return (
        east_face * (padded[..., 2:, :] - middle)
        - west_face * (middle - padded[..., :-2, :])
        + north_face * (jnp.roll(middle, -1, -1) - middle)
        - south_face * (middle - jnp.roll(middle, 1, -1))
    )


def acoustic(grad_x, grad_y):
    dilation = grad_x[..., 1, :, :] + grad_y[..., 2, :, :]
    return jnp.stack(
        [dilation, grad_x[..., 4, :, :], grad_y[..., 4, :, :], jnp.zeros_like(dilation), dilation],
        axis=-3,
    )


def own_terms(middle, grad_x, grad_y, damping, frequency):
    rotation = jnp.stack([-frequency * middle[:, 1], frequency * middle[:, 0]], axis=1)
    return rotation + acoustic(grad_x, grad_y) - damping


def coupling(
    u_real, u_imag, v_real, v_imag, g_real, g_imag, q_real, q_imag, x_real, x_imag, y_real, y_imag
):
    real_part = (
        u_real * x_real
        - u_imag * x_imag
        + v_real * y_real
        - v_imag * y_imag
        + g_real * q_real
        - g_imag * q_imag
    )
    imag_part = (
        u_real * x_imag
        + u_imag * x_real
        + v_real * y_imag
        + v_imag * y_real
        + g_real * q_imag
        + g_imag * q_real
    )
    return (real_part, imag_part)


def block_terms(blocks, middle, grad_x, grad_y):
    local_count = middle.shape[0]
    index_table = np.array(
        [
            [local_count + target - source for source in range(local_count)]
            for target in range(local_count)
        ],
        dtype=np.int32,
    )
    chosen = blocks[index_table]

    def base_part(complex_index, field_index):
        return chosen[:, :, complex_index, field_index][:, :, None]

    def moved_part(values, complex_index):
        return values[None, :, complex_index]

    real_part, imag_part = coupling(
        base_part(0, 0),
        base_part(1, 0),
        base_part(0, 1),
        base_part(1, 1),
        base_part(0, 2),
        base_part(1, 2),
        moved_part(middle, 0),
        moved_part(middle, 1),
        moved_part(grad_x, 0),
        moved_part(grad_x, 1),
        moved_part(grad_y, 0),
        moved_part(grad_y, 1),
    )
    return jnp.stack([jnp.sum(real_part, axis=1), jnp.sum(imag_part, axis=1)], axis=1)


def shards(perturbation, base_flow, viscosity):
    local_count = perturbation.shape[0]
    width_x = perturbation.shape[3]
    width_y = perturbation.shape[4]
    groups = lax.axis_size("harm")
    first_index = lax.axis_index("harm") * local_count
    flattened = perturbation.reshape(local_count * 10, width_x, width_y)
    stacked = jnp.concatenate([flattened, viscosity[None]], axis=0)
    padded = extended(stacked, (("tile", 1),), 1)
    own_padded = padded[:-1].reshape(local_count, 2, 5, width_x + 2, width_y)
    visc_padded = padded[-1]
    numbers = first_index + jnp.arange(local_count, dtype=jnp.int32)
    total_count = local_count * groups
    signed = jnp.where(numbers < total_count // 2, numbers, numbers - total_count)
    frequency = (omega_base * signed.astype(jnp.float32)).reshape(local_count, 1, 1, 1)
    middle, grad_x, grad_y = split_rows(own_padded)
    summed = own_terms(middle, grad_x, grad_y, diffusion(own_padded, visc_padded), frequency)
    whole_base = lax.all_gather(base_flow, "harm", axis=0, tiled=True)

    def base_pair(position, earlier):
        before = lax.dynamic_slice_in_dim(
            whole_base, (position + groups - 1) % groups * local_count, local_count, 0
        )
        current = lax.dynamic_slice_in_dim(whole_base, position * local_count, local_count, 0)
        return (jnp.concatenate([before, current], axis=0), earlier)

    earlier = base_flow
    moving = own_padded

    def advance(moving):
        moved = shifted(moving, "harm", 1)
        return (moved, moved)

    blocks, earlier = base_pair(0, earlier)
    summed = summed + block_terms(blocks, middle, grad_x, grad_y)

    def advance_step(position, carried):
        summed, moving, earlier = carried
        moving, rimmed = advance(moving)
        blocks, earlier = base_pair(position, earlier)
        values, slope_x, slope_y = split_rows(rimmed)
        return (summed + block_terms(blocks, values, slope_x, slope_y), moving, earlier)

    summed, moving, earlier = lax.fori_loop(1, groups, advance_step, (summed, moving, earlier))
    return summed


def ceil_to(count, unit):
    return -(-count // unit) * unit


scoped_bytes = 12 * 1024 * 1024
in_vmem = pl.BlockSpec(memory_space=pltpu.VMEM)
anywhere = pl.BlockSpec(memory_space=pl.ANY)


def lanes_next(value):
    return pltpu.roll(value, value.shape[1] - 1, 1)


def lanes_before(value):
    return pltpu.roll(value, 1, 1)


def rows_next(value, below):
    count = value.shape[0]
    row = lax.broadcasted_iota(jnp.int32, value.shape, 0)
    return jnp.where(row == count - 1, below, pltpu.roll(value, count - 1, 0))


def rows_before(value, above):
    row = lax.broadcasted_iota(jnp.int32, value.shape, 0)
    return jnp.where(row == 0, above, pltpu.roll(value, 1, 0))


class Sizes:
    def __init__(self, perturbation, groups):
        self.local, _, self.fields, self.width, self.columns = perturbation.shape
        self.groups = groups
        self.total = self.local * groups
        self.components = self.local * 2 * self.fields
        self.edge = ceil_to(self.components + 1, 8)
        cut = self.fields - 1
        self.moved, self.sent = (0, cut), (cut, self.fields)
        self.block_rows = self.local * 2 * (self.fields - cut) * self.width
        self.message_rows = ceil_to(self.block_rows + self.local * 2 * cut * 2, 8)

    def at(self, harmonic, part, field):
        return (harmonic * 2 + part) * self.fields + field

    def block(self, harmonic, part, field):
        first, last = self.sent
        start = ((harmonic * 2 + part) * (last - first) + field - first) * self.width
        return slice(start, start + self.width)

    def rim(self, harmonic, part, field, side):
        first, last = self.moved
        at = ((harmonic * 2 + part) * (last - first) + field - first) * 2 + side
        return slice(self.block_rows + at, self.block_rows + at + 1)

    def shape(self, harmonics, fields):
        return (harmonics, 2, fields[1] - fields[0], self.width, self.columns)

    def each(self):
        for harmonic in range(self.local):
            for part in range(2):
                for field in range(self.fields):
                    yield harmonic, part, field


def fetch_kernel(sizes, q_from, visc_from, q_ref, visc_ref, moved_ref, q_sem, visc_sem):
    copies = (
        pltpu.make_async_copy(q_from, q_ref, q_sem),
        pltpu.make_async_copy(visc_from, visc_ref, visc_sem),
    )
    for copy in copies:
        copy.start()
    for copy in copies:
        copy.wait()
    moved_ref[...] = q_ref[:, :, sizes.moved[0] : sizes.moved[1]]


def edge_kernel(row):
    def kernel(sizes, q_ref, visc_ref, *refs):
        edge_ref = refs[-1]
        rows = slice(row, row + 1) if row >= 0 else slice(sizes.width - 1, sizes.width)
        for harmonic, part, field in sizes.each():
            at = sizes.at(harmonic, part, field)
            edge_ref[at : at + 1, :] = q_ref[harmonic, part, field, rows, :]
        at = sizes.components
        edge_ref[at : at + 1, :] = visc_ref[rows, :]
        edge_ref[at + 1 :, :] = jnp.zeros((sizes.edge - at - 1, sizes.columns), jnp.float32)

    return kernel


def halo(sizes, ref, at):
    below = sizes.edge + at
    return ref[at : at + 1, :], ref[below : below + 1, :]


def slope_y(value):
    return 0.5 * (lanes_next(value) - lanes_before(value))


def slope_x(value, above, below):
    return 0.5 * (rows_next(value, below) - rows_before(value, above))


def add_products(sums, chosen, moved):
    real, imag = sums
    for (c_real, c_imag), (m_real, m_imag) in zip(chosen, moved, strict=True):
        more_real = c_real * m_real - c_imag * m_imag
        more_imag = c_real * m_imag + c_imag * m_real
        real = more_real if real is None else real + more_real
        imag = more_imag if imag is None else imag + more_imag
    return real, imag


def chosen_rows(sizes, base, target, source, rows):
    at = lax.rem(target - source + sizes.total, sizes.total)
    return [[base[at, part, term, rows, :] for part in (0, 1)] for term in range(3)]


def result_kernel(sizes, base, q_own, q_core, halo_own, halo_core, out_ref):
    me = lax.axis_index("harm")
    targets = [lax.bitwise_xor(me, 2) * sizes.local + harmonic for harmonic in range(sizes.local)]
    sources = [
        (lax.bitwise_xor(me, place) * sizes.local + harmonic, q_ref, halo_ref, harmonic)
        for place, q_ref, halo_ref in ((0, q_own, halo_own), (1, q_core, halo_core))
        for harmonic in range(sizes.local)
    ]
    first, last = sizes.sent
    parts = (0, 1)
    for field in range(first, last):
        moved = []
        for _, q_ref, halo_ref, harmonic in sources:
            terms = [[], [], []]
            for part in parts:
                value = q_ref[harmonic, part, field]
                above, below = halo(sizes, halo_ref, sizes.at(harmonic, part, field))
                for term, what in zip(
                    terms, (slope_x(value, above, below), slope_y(value), value), strict=True
                ):
                    term.append(what)
            moved.append(terms)
        for start in range(0, sizes.width, 8):
            rows = slice(start, start + 8)
            for harmonic, target in enumerate(targets):
                sums = (None, None)
                for terms, (source, _, _, _) in zip(moved, sources, strict=True):
                    chosen = chosen_rows(sizes, base, target, source, rows)
                    cut = [[value[rows] for value in term] for term in terms]
                    sums = add_products(sums, chosen, cut)
                for part in parts:
                    at = sizes.block(harmonic, part, field).start + start
                    out_ref[at : at + 8, :] = sums[part]
    first, last = sizes.moved
    for side, row, sign in ((0, 0, -0.5), (1, sizes.width - 1, 0.5)):
        outside = [
            [
                jnp.concatenate(
                    [
                        halo(sizes, halo_ref, sizes.at(harmonic, part, field))[side]
                        for field in range(first, last)
                    ],
                    axis=0,
                )
                for part in parts
            ]
            for _, _, halo_ref, harmonic in sources
        ]
        for harmonic, target in enumerate(targets):
            real = imag = 0.0
            for (q_real, q_imag), (source, _, _, _) in zip(outside, sources, strict=True):
                at = lax.rem(target - source + sizes.total, sizes.total)
                u_real = sign * base[at, 0, 0, row : row + 1, :]
                u_imag = sign * base[at, 1, 0, row : row + 1, :]
                real = real + u_real * q_real - u_imag * q_imag
                imag = imag + u_real * q_imag + u_imag * q_real
            for part, value in zip(parts, (real, imag), strict=True):
                for field in range(first, last):
                    at = field - first
                    out_ref[sizes.rim(harmonic, part, field, side), :] = value[at : at + 1, :]
    tail = sizes.block_rows + sizes.local * 2 * (last - first) * 2
    if tail < sizes.message_rows:
        out_ref[tail:, :] = jnp.zeros((sizes.message_rows - tail, sizes.columns), jnp.float32)


def own_terms_into(sizes, q_ref, visc_ref, halo_ref, sum_ref):
    me = lax.axis_index("harm")
    center = visc_ref[...]
    above, below = halo(sizes, halo_ref, sizes.components)
    east = 0.5 * (center + rows_next(center, below))
    west = 0.5 * (center + rows_before(center, above))
    north = 0.5 * (center + lanes_next(center))
    south = 0.5 * (center + lanes_before(center))
    for harmonic in range(sizes.local):
        number = me * sizes.local + harmonic
        signed = jnp.where(number < sizes.total // 2, number, number - sizes.total)
        frequency = omega_base * signed.astype(jnp.float32)
        for part in range(2):
            turn = -frequency if part == 0 else frequency
            terms = {}
            for field in range(sizes.fields):
                value = q_ref[harmonic, part, field]
                above, below = halo(sizes, halo_ref, sizes.at(harmonic, part, field))
                x_next, x_before = rows_next(value, below), rows_before(value, above)
                y_next, y_before = lanes_next(value), lanes_before(value)
                damping = (
                    east * (x_next - value)
                    - west * (value - x_before)
                    + north * (y_next - value)
                    - south * (value - y_before)
                )
                terms[field] = turn * q_ref[harmonic, 1 - part, field] - damping
                if field == 1:
                    dilation = 0.5 * (x_next - x_before)
                elif field == 2:
                    dilation = dilation + 0.5 * (y_next - y_before)
                elif field == 4:
                    terms[1] = terms[1] + 0.5 * (x_next - x_before)
                    terms[2] = terms[2] + 0.5 * (y_next - y_before)
            terms[0] = terms[0] + dilation
            terms[4] = terms[4] + dilation
            for field in range(sizes.fields):
                sum_ref[harmonic, part, field] = terms[field]


def couple(sizes, base, place, fields, start_from, q_ref, halo_ref, slopes, store):
    me = lax.axis_index("harm")
    slopes_x, slopes_y = slopes
    group = lax.bitwise_xor(me, place)
    for field in range(*fields):
        for harmonic in range(sizes.local):
            for part in (0, 1):
                value = q_ref[harmonic, part, field]
                above = below = 0.0
                if halo_ref is not None:
                    above, below = halo(sizes, halo_ref, sizes.at(harmonic, part, field))
                slopes_x[harmonic, part] = slope_x(value, above, below)
                slopes_y[harmonic, part] = slope_y(value)
        for start in range(0, sizes.width, 8):
            rows = slice(start, start + 8)
            sums = [
                [start_from(harmonic, part, field, rows) for part in (0, 1)]
                for harmonic in range(sizes.local)
            ]
            for source in range(sizes.local):
                moved = [
                    [slopes_x[source, part, rows, :] for part in (0, 1)],
                    [slopes_y[source, part, rows, :] for part in (0, 1)],
                    [q_ref[source, part, field, rows, :] for part in (0, 1)],
                ]
                for harmonic in range(sizes.local):
                    target = me * sizes.local + harmonic
                    number = group * sizes.local + source
                    chosen = chosen_rows(sizes, base, target, number, rows)
                    sums[harmonic] = add_products(sums[harmonic], chosen, moved)
            for harmonic in range(sizes.local):
                for part in (0, 1):
                    store(harmonic, part, field, rows, sums[harmonic][part])


def reader(ref):
    return lambda harmonic, part, field, rows: ref[harmonic, part, field, rows, :]


def writer(ref):
    def store(harmonic, part, field, rows, value):
        ref[harmonic, part, field, rows, :] = value

    return store


def own_kernel(
    sizes, base_a, base_b, base_c, base_d, q_ref, halo_ref, visc_ref, sum_ref, base, *slopes
):
    me = lax.axis_index("harm")
    for place, ref in enumerate((base_a, base_b, base_c, base_d)):
        for harmonic in range(sizes.local):
            base[lax.bitwise_xor(me, place) * sizes.local + harmonic] = ref[harmonic]
    own_terms_into(sizes, q_ref, visc_ref, halo_ref, sum_ref)
    everything = (0, sizes.fields)
    couple(
        sizes, base, 0, everything, reader(sum_ref), q_ref, halo_ref, slopes, writer(sum_ref)
    )


def core_kernel(sizes, base, q_ref, halo_ref, before_ref, sum_ref, *slopes):
    everything = (0, sizes.fields)
    couple(
        sizes, base, 1, everything, reader(before_ref), q_ref, halo_ref, slopes, writer(sum_ref)
    )


class Pieces:
    def __init__(self, sizes, refs):
        self.fields = sizes.moved[1]
        self.planes = [(ref, plane) for ref in refs for plane in range(ref.shape[0])]

    def __getitem__(self, at):
        harmonic, part, field, *rest = at
        ref, plane = self.planes[(harmonic * 2 + part) * self.fields + field]
        return ref[(plane, *rest)]


def chip_kernel(sizes, base, q_ref, before_ref, sum_ref, *slopes):
    couple(
        sizes, base, 2, sizes.moved, reader(before_ref), q_ref, None, slopes, writer(sum_ref)
    )


def diag_kernel(sizes, base, before_ref, *refs):
    *values, sum_ref, slopes_x, slopes_y = refs
    values, slopes = Pieces(sizes, values), (slopes_x, slopes_y)
    couple(
        sizes, base, 3, sizes.moved, reader(before_ref), values, None, slopes, writer(sum_ref)
    )


def pass_kernel(sizes, values, after, same):
    pass


def sent_kernel(sizes, near_ref, message, _, sum_ref):
    first = sizes.sent[0]
    for field in range(*sizes.sent):
        for harmonic in range(sizes.local):
            for part in (0, 1):
                more = message[sizes.block(harmonic, part, field), :]
                sum_ref[harmonic, part, field - first] = near_ref[harmonic, part, field] + more


def last_kernel(sizes, sent_ref, far_ref, message, out_ref, result, sems):
    copies = []

    def send(source, field):
        copies.append(pltpu.make_async_copy(source, out_ref.at[:, :, field], sems.at[field]))
        copies[-1].start()

    for field in range(*sizes.sent):
        send(sent_ref.at[:, :, field - sizes.sent[0]], field)
    for field in range(*sizes.moved):
        for harmonic in range(sizes.local):
            for part in (0, 1):
                result[harmonic, part, field] = far_ref[harmonic, part, field]
                for side, row in ((0, 0), (1, sizes.width - 1)):
                    more = message[sizes.rim(harmonic, part, field, side), :]
                    result[harmonic, part, field, row : row + 1, :] += more
        send(result.at[:, :, field], field)
    for copy in copies:
        copy.wait()


def paired_shards(perturbation, base_flow, viscosity):
    groups, tiles = lax.axis_size("harm"), lax.axis_size("tile")
    sizes = Sizes(perturbation, groups)

    def to_chip(value):
        return lax.ppermute(value, "harm", [(i, i ^ 2) for i in range(groups)])

    def to_core(value):
        return lax.ppermute(value, "harm", [(i, i ^ 1) for i in range(groups)])

    def along_tile(value, step):
        return lax.ppermute(value, "tile", [(i, (i + step) % tiles) for i in range(tiles)])

    def array(*shape):
        return jax.ShapeDtypeStruct(shape, jnp.float32)

    def call(
        kernel, operands, outs, scratch=(), in_specs=None, out_specs=None, flops=1, aliases=None
    ):
        return pl.pallas_call(
            functools.partial(kernel, sizes),
            in_specs=in_specs or [in_vmem] * len(operands),
            out_shape=outs,
            out_specs=out_specs or [in_vmem] * len(outs),
            scratch_shapes=scratch,
            input_output_aliases=aliases or {},
            cost_estimate=pl.CostEstimate(flops=flops, bytes_accessed=1, transcendentals=0),
            compiler_params=pltpu.CompilerParams(vmem_limit_bytes=scoped_bytes),
        )(*operands)

    slopes = [pltpu.VMEM((sizes.local, 2, sizes.width, sizes.columns), jnp.float32)] * 2
    edges = array(sizes.edge, sizes.columns)

    base_chip = to_chip(base_flow)
    held, visc, moved = call(
        fetch_kernel,
        [pltpu.with_memory_space_constraint(x, pltpu.HBM) for x in (perturbation, viscosity)],
        [
            array(*perturbation.shape),
            array(*viscosity.shape),
            array(*sizes.shape(sizes.local, sizes.moved)),
        ],
        [pltpu.SemaphoreType.DMA] * 2,
        [anywhere] * 2,
    )
    up = call(edge_kernel(-1), (held, visc), [edges])[0]
    base_core = to_core(base_flow)
    above = along_tile(up, 1)
    moved_chip = to_chip(moved)
    down = call(
        edge_kernel(0), (held, visc, base_core), [edges], in_specs=[in_vmem] * 2 + [anywhere]
    )[0]
    below = along_tile(down, -1)
    halo_own = jnp.concatenate([above, below], axis=0)
    halo_core = to_core(halo_own)
    held_core = to_core(perturbation)
    base_diag = to_core(base_chip)
    own_sum, base = call(
        own_kernel,
        (base_flow, base_core, base_chip, base_diag, held, halo_own, visc),
        [array(*perturbation.shape), array(sizes.total, *base_flow.shape[1:])],
        slopes,
    )
    message = call(
        result_kernel,
        (base, held, held_core, halo_own, halo_core),
        [array(sizes.message_rows, sizes.columns)],
    )[0]
    results = to_chip(message)
    near_sum = call(
        core_kernel, (base, held_core, halo_core, own_sum), [array(*perturbation.shape)], slopes
    )[0]
    moved_here = call(
        pass_kernel,
        (moved_chip, near_sum),
        array(*moved_chip.shape),
        in_specs=[anywhere] * 2,
        out_specs=anywhere,
        flops=1,
        aliases={0: 0},
    )
    flat = moved_here.reshape(-1, sizes.width, sizes.columns)
    starts = [len(flat) * place // 3 for place in range(3 + 1)]
    pieces = [to_core(flat[begin:end]) for begin, end in zip(starts, starts[1:])]
    far_sum = call(
        chip_kernel,
        (base, moved_here, near_sum),
        [array(*sizes.shape(sizes.local, sizes.moved))],
        slopes,
    )[0]
    far_sum = call(
        diag_kernel,
        (base, far_sum, *pieces),
        [array(*sizes.shape(sizes.local, sizes.moved))],
        slopes,
    )[0]
    sent_sum = call(
        sent_kernel,
        (near_sum, results, far_sum),
        [array(*sizes.shape(sizes.local, sizes.sent))],
        flops=3*10**9,
        in_specs=[in_vmem, in_vmem, anywhere],
    )[0]
    return call(
        last_kernel,
        (sent_sum, far_sum, results),
        array(*perturbation.shape),
        [
            pltpu.VMEM(sizes.shape(sizes.local, sizes.moved), jnp.float32),
            pltpu.SemaphoreType.DMA((sizes.fields,)),
        ],
        out_specs=anywhere,
    )


def solution(mesh):
    placed = (
        P("harm", None, None, ("parts", "tile"), None),
        P("harm", None, None, ("parts", "tile"), None),
        P(("parts", "tile"), None),
    )

    def chosen(perturbation, base_flow, viscosity):
        two_chips = mesh.shape["harm"] == 2 * 2
        whole_tiles = perturbation.shape[3] % 8 == 0 and perturbation.shape[4] % 128 == 0
        body = paired_shards if two_chips and whole_tiles else shards
        return body(perturbation, base_flow, viscosity)

    return jax.shard_map(
        chosen,
        mesh=mesh,
        in_specs=placed,
        out_specs=P("harm", None, None, ("parts", "tile"), None),
        check_vma=False,
    )
```

```python
import functools

import jax
import jax.numpy as jnp
import numpy as np
from jax import lax
from jax.experimental import pallas as pl
from jax.experimental.pallas import tpu as pltpu
from jax.sharding import PartitionSpec as P

omega_base = 0.25


def extended(cells, sides, width):
    for axis, dim in sides:
        count = lax.axis_size(axis)
        head = lax.slice_in_dim(cells, 0, width, axis=dim)
        tail = lax.slice_in_dim(cells, cells.shape[dim] - width, cells.shape[dim], axis=dim)
        cells = jnp.concatenate(
            [
                lax.ppermute(tail, axis, [(i, (i + 1) % count) for i in range(count)]),
                cells,
                lax.ppermute(head, axis, [((i + 1) % count, i) for i in range(count)]),
            ],
            axis=dim,
        )
    return cells


def shifted(value, axis, steps):
    count = lax.axis_size(axis)
    pairs = [(source, (source + steps) % count) for source in range(count)]
    return lax.ppermute(value, axis, pairs)


def split_rows(padded):
    middle = padded[..., 1:-1, :]
    grad_x = 0.5 * (padded[..., 2:, :] - padded[..., :-2, :])
    grad_y = 0.5 * (jnp.roll(middle, -1, -1) - jnp.roll(middle, 1, -1))
    return (middle, grad_x, grad_y)


def diffusion(padded, visc_padded):
    middle = padded[..., 1:-1, :]
    center = visc_padded[1:-1]
    east_face = 0.5 * (center + visc_padded[2:])
    west_face = 0.5 * (center + visc_padded[:-2])
    north_face = 0.5 * (center + jnp.roll(center, -1, -1))
    south_face = 0.5 * (center + jnp.roll(center, 1, -1))
    return (
        east_face * (padded[..., 2:, :] - middle)
        - west_face * (middle - padded[..., :-2, :])
        + north_face * (jnp.roll(middle, -1, -1) - middle)
        - south_face * (middle - jnp.roll(middle, 1, -1))
    )


def acoustic(grad_x, grad_y):
    dilation = grad_x[..., 1, :, :] + grad_y[..., 2, :, :]
    return jnp.stack(
        [dilation, grad_x[..., 4, :, :], grad_y[..., 4, :, :], jnp.zeros_like(dilation), dilation],
        axis=-3,
    )


def own_terms(middle, grad_x, grad_y, damping, frequency):
    rotation = jnp.stack([-frequency * middle[:, 1], frequency * middle[:, 0]], axis=1)
    return rotation + acoustic(grad_x, grad_y) - damping


def coupling(
    u_real, u_imag, v_real, v_imag, g_real, g_imag, q_real, q_imag, x_real, x_imag, y_real, y_imag
):
    real_part = (
        u_real * x_real
        - u_imag * x_imag
        + v_real * y_real
        - v_imag * y_imag
        + g_real * q_real
        - g_imag * q_imag
    )
    imag_part = (
        u_real * x_imag
        + u_imag * x_real
        + v_real * y_imag
        + v_imag * y_real
        + g_real * q_imag
        + g_imag * q_real
    )
    return (real_part, imag_part)


def block_terms(blocks, middle, grad_x, grad_y):
    local_count = middle.shape[0]
    index_table = np.array(
        [
            [local_count + target - source for source in range(local_count)]
            for target in range(local_count)
        ],
        dtype=np.int32,
    )
    chosen = blocks[index_table]

    def base_part(complex_index, field_index):
        return chosen[:, :, complex_index, field_index][:, :, None]

    def moved_part(values, complex_index):
        return values[None, :, complex_index]

    real_part, imag_part = coupling(
        base_part(0, 0),
        base_part(1, 0),
        base_part(0, 1),
        base_part(1, 1),
        base_part(0, 2),
        base_part(1, 2),
        moved_part(middle, 0),
        moved_part(middle, 1),
        moved_part(grad_x, 0),
        moved_part(grad_x, 1),
        moved_part(grad_y, 0),
        moved_part(grad_y, 1),
    )
    return jnp.stack([jnp.sum(real_part, axis=1), jnp.sum(imag_part, axis=1)], axis=1)


def shards(perturbation, base_flow, viscosity):
    local_count = perturbation.shape[0]
    width_x = perturbation.shape[3]
    width_y = perturbation.shape[4]
    groups = lax.axis_size("harm")
    first_index = lax.axis_index("harm") * local_count
    flattened = perturbation.reshape(local_count * 10, width_x, width_y)
    stacked = jnp.concatenate([flattened, viscosity[None]], axis=0)
    padded = extended(stacked, (("tile", 1),), 1)
    own_padded = padded[:-1].reshape(local_count, 2, 5, width_x + 2, width_y)
    visc_padded = padded[-1]
    numbers = first_index + jnp.arange(local_count, dtype=jnp.int32)
    total_count = local_count * groups
    signed = jnp.where(numbers < total_count // 2, numbers, numbers - total_count)
    frequency = (omega_base * signed.astype(jnp.float32)).reshape(local_count, 1, 1, 1)
    middle, grad_x, grad_y = split_rows(own_padded)
    summed = own_terms(middle, grad_x, grad_y, diffusion(own_padded, visc_padded), frequency)
    whole_base = lax.all_gather(base_flow, "harm", axis=0, tiled=True)

    def base_pair(position, earlier):
        before = lax.dynamic_slice_in_dim(
            whole_base, (position + groups - 1) % groups * local_count, local_count, 0
        )
        current = lax.dynamic_slice_in_dim(whole_base, position * local_count, local_count, 0)
        return (jnp.concatenate([before, current], axis=0), earlier)

    earlier = base_flow
    moving = own_padded

    def advance(moving):
        moved = shifted(moving, "harm", 1)
        return (moved, moved)

    blocks, earlier = base_pair(0, earlier)
    summed = summed + block_terms(blocks, middle, grad_x, grad_y)

    def advance_step(position, carried):
        summed, moving, earlier = carried
        moving, rimmed = advance(moving)
        blocks, earlier = base_pair(position, earlier)
        values, slope_x, slope_y = split_rows(rimmed)
        return (summed + block_terms(blocks, values, slope_x, slope_y), moving, earlier)

    summed, moving, earlier = lax.fori_loop(1, groups, advance_step, (summed, moving, earlier))
    return summed


def ceil_to(count, unit):
    return -(-count // unit) * unit


scoped_bytes = 12 * 1024 * 1024
results_flops = 3 * 10**9
hand_on_pieces = 3
in_vmem = pl.BlockSpec(memory_space=pltpu.VMEM)
anywhere = pl.BlockSpec(memory_space=pl.ANY)


def lanes_next(value):
    return pltpu.roll(value, value.shape[1] - 1, 1)


def lanes_before(value):
    return pltpu.roll(value, 1, 1)


def rows_next(value, below):
    count = value.shape[0]
    row = lax.broadcasted_iota(jnp.int32, value.shape, 0)
    return jnp.where(row == count - 1, below, pltpu.roll(value, count - 1, 0))


def rows_before(value, above):
    row = lax.broadcasted_iota(jnp.int32, value.shape, 0)
    return jnp.where(row == 0, above, pltpu.roll(value, 1, 0))


class Sizes:
    def __init__(self, perturbation, groups):
        self.local, _, self.fields, self.width, self.columns = perturbation.shape
        self.groups = groups
        self.total = self.local * groups
        self.components = self.local * 2 * self.fields
        self.edge = ceil_to(self.components + 1, 8)
        cut = self.fields - 1
        self.moved, self.sent = (0, cut), (cut, self.fields)
        self.block_rows = self.local * 2 * (self.fields - cut) * self.width
        self.message_rows = ceil_to(self.block_rows + self.local * 2 * cut * 2, 8)

    def at(self, harmonic, part, field):
        return (harmonic * 2 + part) * self.fields + field

    def block(self, harmonic, part, field):
        first, last = self.sent
        start = ((harmonic * 2 + part) * (last - first) + field - first) * self.width
        return slice(start, start + self.width)

    def rim(self, harmonic, part, field, side):
        first, last = self.moved
        at = ((harmonic * 2 + part) * (last - first) + field - first) * 2 + side
        return slice(self.block_rows + at, self.block_rows + at + 1)

    def shape(self, harmonics, fields):
        return (harmonics, 2, fields[1] - fields[0], self.width, self.columns)

    def each(self):
        for harmonic in range(self.local):
            for part in range(2):
                for field in range(self.fields):
                    yield harmonic, part, field


def fetch_kernel(sizes, q_from, visc_from, q_ref, visc_ref, moved_ref, q_sem, visc_sem):
    copies = (
        pltpu.make_async_copy(q_from, q_ref, q_sem),
        pltpu.make_async_copy(visc_from, visc_ref, visc_sem),
    )
    for copy in copies:
        copy.start()
    for copy in copies:
        copy.wait()
    moved_ref[...] = q_ref[:, :, sizes.moved[0] : sizes.moved[1]]


def edge_kernel(row):
    def kernel(sizes, q_ref, visc_ref, *refs):
        edge_ref = refs[-1]
        rows = slice(row, row + 1) if row >= 0 else slice(sizes.width - 1, sizes.width)
        for harmonic, part, field in sizes.each():
            at = sizes.at(harmonic, part, field)
            edge_ref[at : at + 1, :] = q_ref[harmonic, part, field, rows, :]
        at = sizes.components
        edge_ref[at : at + 1, :] = visc_ref[rows, :]
        edge_ref[at + 1 :, :] = jnp.zeros((sizes.edge - at - 1, sizes.columns), jnp.float32)

    return kernel


def halo(ref, sizes, harmonic, part, field):
    at = sizes.at(harmonic, part, field)
    return halo_rows(ref, sizes, at)


def halo_rows(ref, sizes, at):
    return tuple(ref[start : start + 1, :] for start in (at, sizes.edge + at))


def slope_y(value):
    return 0.5 * (lanes_next(value) - lanes_before(value))


def slope_x(value, above, below):
    return 0.5 * (rows_next(value, below) - rows_before(value, above))


def add_products(sums, chosen, moved):
    real, imag = sums
    for (c_real, c_imag), (m_real, m_imag) in zip(chosen, moved, strict=True):
        more_real = c_real * m_real - c_imag * m_imag
        more_imag = c_real * m_imag + c_imag * m_real
        real = more_real if real is None else real + more_real
        imag = more_imag if imag is None else imag + more_imag
    return real, imag


def chosen_rows(sizes, base, target, source, rows):
    at = lax.rem(target - source + sizes.total, sizes.total)
    return [[base[at, part, term, rows, :] for part in (0, 1)] for term in range(3)]


def chip_sources(sizes):
    me = lax.axis_index("harm")
    return [
        (lax.bitwise_xor(me, place) * sizes.local + harmonic, place, harmonic)
        for place in (0, 1)
        for harmonic in range(sizes.local)
    ]


def far_targets(sizes):
    me = lax.axis_index("harm")
    return [lax.bitwise_xor(me, 2) * sizes.local + harmonic for harmonic in range(sizes.local)]


def block_into(sizes, base, q_own, q_core, block_ref):
    sources = chip_sources(sizes)
    for field in range(*sizes.sent):
        moved = []
        for _, place, harmonic in sources:
            parts = [(q_own, q_core)[place][harmonic, part, field] for part in (0, 1)]
            moved.append(
                [
                    [slope_x(value, 0.0, 0.0) for value in parts],
                    [slope_y(value) for value in parts],
                    parts,
                ]
            )
        for start in range(0, sizes.width, 8):
            rows = slice(start, start + 8)
            for harmonic, target in enumerate(far_targets(sizes)):
                sums = (None, None)
                for terms, (source, _, _) in zip(moved, sources, strict=True):
                    chosen = chosen_rows(sizes, base, target, source, rows)
                    cut = [[value[rows] for value in term] for term in terms]
                    sums = add_products(sums, chosen, cut)
                for part in (0, 1):
                    at = sizes.block(harmonic, part, field).start + start
                    block_ref[at : at + 8, :] = sums[part]


def result_kernel(sizes, base, block_ref, halo_own, halo_core, out_ref):
    out_ref[: sizes.block_rows, :] = block_ref[...]
    sources = chip_sources(sizes)
    for side, row, sign in ((0, 0, -0.5), (1, sizes.width - 1, 0.5)):
        outside = [
            [
                jnp.concatenate(
                    [
                        halo((halo_own, halo_core)[place], sizes, harmonic, part, field)[side]
                        for field in range(sizes.fields)
                    ],
                    axis=0,
                )
                for part in (0, 1)
            ]
            for _, place, harmonic in sources
        ]
        for harmonic, target in enumerate(far_targets(sizes)):
            real = imag = 0.0
            for (q_real, q_imag), (source, _, _) in zip(outside, sources, strict=True):
                at = lax.rem(target - source + sizes.total, sizes.total)
                u_real = sign * base[at, 0, 0, row : row + 1, :]
                u_imag = sign * base[at, 1, 0, row : row + 1, :]
                real = real + u_real * q_real - u_imag * q_imag
                imag = imag + u_real * q_imag + u_imag * q_real
            for part, value in zip((0, 1), (real, imag), strict=True):
                for field in range(sizes.fields):
                    more = value[field : field + 1, :]
                    if field < sizes.moved[1]:
                        out_ref[sizes.rim(harmonic, part, field, side), :] = more
                    else:
                        at = sizes.block(harmonic, part, field).start + row
                        out_ref[at : at + 1, :] += more
    tail = sizes.block_rows + sizes.local * 2 * (sizes.moved[1] - sizes.moved[0]) * 2
    if tail < sizes.message_rows:
        out_ref[tail:, :] = jnp.zeros((sizes.message_rows - tail, sizes.columns), jnp.float32)


def own_terms_into(sizes, q_ref, visc_ref, halo_ref, sum_ref):
    me = lax.axis_index("harm")
    center = visc_ref[...]
    above, below = halo_rows(halo_ref, sizes, sizes.components)
    east = 0.5 * (center + rows_next(center, below))
    west = 0.5 * (center + rows_before(center, above))
    north = 0.5 * (center + lanes_next(center))
    south = 0.5 * (center + lanes_before(center))
    for harmonic in range(sizes.local):
        number = me * sizes.local + harmonic
        signed = jnp.where(number < sizes.total // 2, number, number - sizes.total)
        frequency = omega_base * signed.astype(jnp.float32)
        for part in range(2):
            turn = -frequency if part == 0 else frequency
            terms = {}
            for field in range(sizes.fields):
                value = q_ref[harmonic, part, field]
                above, below = halo(halo_ref, sizes, harmonic, part, field)
                x_next, x_before = rows_next(value, below), rows_before(value, above)
                y_next, y_before = lanes_next(value), lanes_before(value)
                damping = (
                    east * (x_next - value)
                    - west * (value - x_before)
                    + north * (y_next - value)
                    - south * (value - y_before)
                )
                terms[field] = turn * q_ref[harmonic, 1 - part, field] - damping
                if field == 1:
                    dilation = 0.5 * (x_next - x_before)
                elif field == 2:
                    dilation = dilation + 0.5 * (y_next - y_before)
                elif field == 4:
                    terms[1] = terms[1] + 0.5 * (x_next - x_before)
                    terms[2] = terms[2] + 0.5 * (y_next - y_before)
            terms[0] = terms[0] + dilation
            terms[4] = terms[4] + dilation
            for field in range(sizes.fields):
                sum_ref[harmonic, part, field] = terms[field]


def couple(sizes, base, place, fields, start_from, q_ref, halo_ref, slopes, store):
    me = lax.axis_index("harm")
    slopes_x, slopes_y = slopes
    group = lax.bitwise_xor(me, place)
    for field in range(*fields):
        for harmonic in range(sizes.local):
            for part in (0, 1):
                value = q_ref[harmonic, part, field]
                above = below = 0.0
                if halo_ref is not None:
                    above, below = halo(halo_ref, sizes, harmonic, part, field)
                slopes_x[harmonic, part] = slope_x(value, above, below)
                slopes_y[harmonic, part] = slope_y(value)
        for start in range(0, sizes.width, 8):
            rows = slice(start, start + 8)
            sums = [
                [start_from(harmonic, part, field, rows) for part in (0, 1)]
                for harmonic in range(sizes.local)
            ]
            for source in range(sizes.local):
                moved = [
                    [slopes_x[source, part, rows, :] for part in (0, 1)],
                    [slopes_y[source, part, rows, :] for part in (0, 1)],
                    [q_ref[source, part, field, rows, :] for part in (0, 1)],
                ]
                for harmonic in range(sizes.local):
                    target = me * sizes.local + harmonic
                    number = group * sizes.local + source
                    chosen = chosen_rows(sizes, base, target, number, rows)
                    sums[harmonic] = add_products(sums[harmonic], chosen, moved)
            for harmonic in range(sizes.local):
                for part in (0, 1):
                    store(harmonic, part, field, rows, sums[harmonic][part])


def reader(ref):
    return lambda harmonic, part, field, rows: ref[harmonic, part, field, rows, :]


def writer(ref):
    def store(harmonic, part, field, rows, value):
        ref[harmonic, part, field, rows, :] = value

    return store


def own_kernel(
    sizes, base_a, base_b, base_c, base_d, q_own, q_core, halo_ref, visc_ref, sum_ref, base, block_ref,
    *slopes,
):
    me = lax.axis_index("harm")
    for place, ref in enumerate((base_a, base_b, base_c, base_d)):
        for harmonic in range(sizes.local):
            base[lax.bitwise_xor(me, place) * sizes.local + harmonic] = ref[harmonic]
    block_into(sizes, base, q_own, q_core, block_ref)
    own_terms_into(sizes, q_own, visc_ref, halo_ref, sum_ref)
    everything = (0, sizes.fields)
    couple(sizes, base, 0, everything, reader(sum_ref), q_own, halo_ref, slopes, writer(sum_ref))


def core_kernel(sizes, base, q_ref, halo_ref, before_ref, sum_ref, *slopes):
    everything = (0, sizes.fields)
    couple(sizes, base, 1, everything, reader(before_ref), q_ref, halo_ref, slopes, writer(sum_ref))


class Pieces:
    def __init__(self, sizes, refs):
        self.sizes = sizes
        self.blocks = [
            (ref, slice(start, start + 8)) for ref in refs for start in range(0, ref.shape[0], 8)
        ]

    def __getitem__(self, at):
        harmonic, part, field, *rest = at
        plane = (harmonic * 2 + part) * self.sizes.moved[1] + field
        count = self.sizes.width // 8
        chosen = range(rest[0].start // 8, rest[0].stop // 8) if rest else range(count)
        blocks = [self.blocks[plane * count + block] for block in chosen]
        return jnp.concatenate([ref[rows, :] for ref, rows in blocks], axis=0)


def chip_kernel(sizes, base, q_ref, before_ref, sum_ref, *slopes):
    couple(
        sizes, base, 2, sizes.moved, reader(before_ref), q_ref, None, slopes, writer(sum_ref)
    )


def diag_kernel(sizes, base, before_ref, *refs):
    *values, sum_ref, slopes_x, slopes_y = refs
    values, slopes = Pieces(sizes, values), (slopes_x, slopes_y)
    couple(
        sizes, base, 3, sizes.moved, reader(before_ref), values, None, slopes, writer(sum_ref)
    )


def pass_kernel(sizes, values, after, same):
    pass


def sent_kernel(sizes, near_ref, message, _, sum_ref):
    first = sizes.sent[0]
    for field in range(*sizes.sent):
        for harmonic in range(sizes.local):
            for part in (0, 1):
                more = message[sizes.block(harmonic, part, field), :]
                sum_ref[harmonic, part, field - first] = near_ref[harmonic, part, field] + more


def last_kernel(sizes, sent_ref, far_ref, message, out_ref, result, sems):
    copies = []

    def send(source, field):
        copies.append(pltpu.make_async_copy(source, out_ref.at[:, :, field], sems.at[field]))
        copies[-1].start()

    for field in range(*sizes.sent):
        send(sent_ref.at[:, :, field - sizes.sent[0]], field)
    for field in range(*sizes.moved):
        for harmonic in range(sizes.local):
            for part in (0, 1):
                result[harmonic, part, field] = far_ref[harmonic, part, field]
                for side, row in ((0, 0), (1, sizes.width - 1)):
                    more = message[sizes.rim(harmonic, part, field, side), :]
                    result[harmonic, part, field, row : row + 1, :] += more
        send(result.at[:, :, field], field)
    for copy in copies:
        copy.wait()


def paired_shards(perturbation, base_flow, viscosity):
    groups, tiles = lax.axis_size("harm"), lax.axis_size("tile")
    sizes = Sizes(perturbation, groups)

    def to_chip(value):
        return lax.ppermute(value, "harm", [(i, i ^ 2) for i in range(groups)])

    def to_core(value):
        return lax.ppermute(value, "harm", [(i, i ^ 1) for i in range(groups)])

    def along_tile(value, step):
        return lax.ppermute(value, "tile", [(i, (i + step) % tiles) for i in range(tiles)])

    def array(*shape):
        return jax.ShapeDtypeStruct(shape, jnp.float32)

    def call(
        kernel, operands, outs, scratch=(), in_specs=None, out_specs=None, flops=1, aliases=None
    ):
        return pl.pallas_call(
            functools.partial(kernel, sizes),
            in_specs=in_specs or [in_vmem] * len(operands),
            out_shape=outs,
            out_specs=out_specs or [in_vmem] * len(outs),
            scratch_shapes=scratch,
            input_output_aliases=aliases or {},
            cost_estimate=pl.CostEstimate(flops=flops, bytes_accessed=1, transcendentals=0),
            compiler_params=pltpu.CompilerParams(vmem_limit_bytes=scoped_bytes),
        )(*operands)

    slopes = [pltpu.VMEM((sizes.local, 2, sizes.width, sizes.columns), jnp.float32)] * 2
    edges = array(sizes.edge, sizes.columns)

    base_chip = to_chip(base_flow)
    held, visc, moved = call(
        fetch_kernel,
        [pltpu.with_memory_space_constraint(x, pltpu.HBM) for x in (perturbation, viscosity)],
        [
            array(*perturbation.shape),
            array(*viscosity.shape),
            array(*sizes.shape(sizes.local, sizes.moved)),
        ],
        [pltpu.SemaphoreType.DMA] * 2,
        [anywhere] * 2,
    )
    up = call(edge_kernel(-1), (held, visc), [edges])[0]
    base_core = to_core(base_flow)
    above = along_tile(up, 1)
    moved_chip = to_chip(moved)
    down = call(
        edge_kernel(0), (held, visc, base_core), [edges], in_specs=[in_vmem] * 2 + [anywhere]
    )[0]
    below = along_tile(down, -1)
    halo_own = jnp.concatenate([above, below], axis=0)
    halo_core = to_core(halo_own)
    held_core = to_core(perturbation)
    base_diag = to_core(base_chip)
    own_sum, base, block = call(
        own_kernel,
        (base_flow, base_core, base_chip, base_diag, held, held_core, halo_own, visc),
        [
            array(*perturbation.shape),
            array(sizes.total, *base_flow.shape[1:]),
            array(sizes.block_rows, sizes.columns),
        ],
        slopes,
    )
    message = call(
        result_kernel,
        (base, block, halo_own, halo_core),
        [array(sizes.message_rows, sizes.columns)],
    )[0]
    results = to_chip(message)
    near_sum = call(
        core_kernel, (base, held_core, halo_core, own_sum), [array(*perturbation.shape)], slopes
    )[0]
    moved_here = call(
        pass_kernel,
        (moved_chip, near_sum),
        array(*moved_chip.shape),
        in_specs=[anywhere] * 2,
        out_specs=anywhere,
        flops=1,
        aliases={0: 0},
    )
    flat = moved_here.reshape(-1, sizes.columns)
    starts = [len(flat) // 8 * place // hand_on_pieces * 8 for place in range(hand_on_pieces + 1)]
    pieces = [to_core(flat[begin:end]) for begin, end in zip(starts, starts[1:])]
    far_sum = call(
        chip_kernel,
        (base, moved_here, near_sum),
        [array(*sizes.shape(sizes.local, sizes.moved))],
        slopes,
    )[0]
    far_sum = call(
        diag_kernel,
        (base, far_sum, *pieces),
        [array(*sizes.shape(sizes.local, sizes.moved))],
        slopes,
    )[0]
    sent_sum = call(
        sent_kernel,
        (near_sum, results, far_sum),
        [array(*sizes.shape(sizes.local, sizes.sent))],
        flops=results_flops,
        in_specs=[in_vmem, in_vmem, anywhere],
    )[0]
    return call(
        last_kernel,
        (sent_sum, far_sum, results),
        array(*perturbation.shape),
        [
            pltpu.VMEM(sizes.shape(sizes.local, sizes.moved), jnp.float32),
            pltpu.SemaphoreType.DMA((sizes.fields,)),
        ],
        out_specs=anywhere,
    )


def solution(mesh):
    placed = (
        P("harm", None, None, ("parts", "tile"), None),
        P("harm", None, None, ("parts", "tile"), None),
        P(("parts", "tile"), None),
    )

    def chosen(perturbation, base_flow, viscosity):
        two_chips = mesh.shape["harm"] == 2 * 2
        whole_tiles = perturbation.shape[3] % 8 == 0 and perturbation.shape[4] % 128 == 0
        body = paired_shards if two_chips and whole_tiles else shards
        return body(perturbation, base_flow, viscosity)

    return jax.shard_map(
        chosen,
        mesh=mesh,
        in_specs=placed,
        out_specs=P("harm", None, None, ("parts", "tile"), None),
        check_vma=False,
    )
```

```python
import functools

import jax
import jax.numpy as jnp
import numpy as np
from jax import lax
from jax.experimental import pallas as pl
from jax.experimental.pallas import tpu as pltpu
from jax.sharding import PartitionSpec as P

omega_base = 0.25


def extended(cells, sides, width):
    for axis, dim in sides:
        count = lax.axis_size(axis)
        head = lax.slice_in_dim(cells, 0, width, axis=dim)
        tail = lax.slice_in_dim(cells, cells.shape[dim] - width, cells.shape[dim], axis=dim)
        cells = jnp.concatenate(
            [
                lax.ppermute(tail, axis, [(i, (i + 1) % count) for i in range(count)]),
                cells,
                lax.ppermute(head, axis, [((i + 1) % count, i) for i in range(count)]),
            ],
            axis=dim,
        )
    return cells


def shifted(value, axis, steps):
    count = lax.axis_size(axis)
    pairs = [(source, (source + steps) % count) for source in range(count)]
    return lax.ppermute(value, axis, pairs)


def split_rows(padded):
    middle = padded[..., 1:-1, :]
    grad_x = 0.5 * (padded[..., 2:, :] - padded[..., :-2, :])
    grad_y = 0.5 * (jnp.roll(middle, -1, -1) - jnp.roll(middle, 1, -1))
    return (middle, grad_x, grad_y)


def diffusion(padded, visc_padded):
    middle = padded[..., 1:-1, :]
    center = visc_padded[1:-1]
    east_face = 0.5 * (center + visc_padded[2:])
    west_face = 0.5 * (center + visc_padded[:-2])
    north_face = 0.5 * (center + jnp.roll(center, -1, -1))
    south_face = 0.5 * (center + jnp.roll(center, 1, -1))
    return (
        east_face * (padded[..., 2:, :] - middle)
        - west_face * (middle - padded[..., :-2, :])
        + north_face * (jnp.roll(middle, -1, -1) - middle)
        - south_face * (middle - jnp.roll(middle, 1, -1))
    )


def acoustic(grad_x, grad_y):
    dilation = grad_x[..., 1, :, :] + grad_y[..., 2, :, :]
    return jnp.stack(
        [dilation, grad_x[..., 4, :, :], grad_y[..., 4, :, :], jnp.zeros_like(dilation), dilation],
        axis=-3,
    )


def own_terms(middle, grad_x, grad_y, damping, frequency):
    rotation = jnp.stack([-frequency * middle[:, 1], frequency * middle[:, 0]], axis=1)
    return rotation + acoustic(grad_x, grad_y) - damping


def coupling(
    u_real, u_imag, v_real, v_imag, g_real, g_imag, q_real, q_imag, x_real, x_imag, y_real, y_imag
):
    real_part = (
        u_real * x_real
        - u_imag * x_imag
        + v_real * y_real
        - v_imag * y_imag
        + g_real * q_real
        - g_imag * q_imag
    )
    imag_part = (
        u_real * x_imag
        + u_imag * x_real
        + v_real * y_imag
        + v_imag * y_real
        + g_real * q_imag
        + g_imag * q_real
    )
    return (real_part, imag_part)


def block_terms(blocks, middle, grad_x, grad_y):
    local_count = middle.shape[0]
    index_table = np.array(
        [
            [local_count + target - source for source in range(local_count)]
            for target in range(local_count)
        ],
        dtype=np.int32,
    )
    chosen = blocks[index_table]

    def base_part(complex_index, field_index):
        return chosen[:, :, complex_index, field_index][:, :, None]

    def moved_part(values, complex_index):
        return values[None, :, complex_index]

    real_part, imag_part = coupling(
        base_part(0, 0),
        base_part(1, 0),
        base_part(0, 1),
        base_part(1, 1),
        base_part(0, 2),
        base_part(1, 2),
        moved_part(middle, 0),
        moved_part(middle, 1),
        moved_part(grad_x, 0),
        moved_part(grad_x, 1),
        moved_part(grad_y, 0),
        moved_part(grad_y, 1),
    )
    return jnp.stack([jnp.sum(real_part, axis=1), jnp.sum(imag_part, axis=1)], axis=1)


def shards(perturbation, base_flow, viscosity):
    local_count = perturbation.shape[0]
    width_x = perturbation.shape[3]
    width_y = perturbation.shape[4]
    groups = lax.axis_size("harm")
    first_index = lax.axis_index("harm") * local_count
    flattened = perturbation.reshape(local_count * 10, width_x, width_y)
    stacked = jnp.concatenate([flattened, viscosity[None]], axis=0)
    padded = extended(stacked, (("tile", 1),), 1)
    own_padded = padded[:-1].reshape(local_count, 2, 5, width_x + 2, width_y)
    visc_padded = padded[-1]
    numbers = first_index + jnp.arange(local_count, dtype=jnp.int32)
    total_count = local_count * groups
    signed = jnp.where(numbers < total_count // 2, numbers, numbers - total_count)
    frequency = (omega_base * signed.astype(jnp.float32)).reshape(local_count, 1, 1, 1)
    middle, grad_x, grad_y = split_rows(own_padded)
    summed = own_terms(middle, grad_x, grad_y, diffusion(own_padded, visc_padded), frequency)
    whole_base = lax.all_gather(base_flow, "harm", axis=0, tiled=True)

    def base_pair(position, earlier):
        before = lax.dynamic_slice_in_dim(
            whole_base, (position + groups - 1) % groups * local_count, local_count, 0
        )
        current = lax.dynamic_slice_in_dim(whole_base, position * local_count, local_count, 0)
        return (jnp.concatenate([before, current], axis=0), earlier)

    earlier = base_flow
    moving = own_padded

    def advance(moving):
        moved = shifted(moving, "harm", 1)
        return (moved, moved)

    blocks, earlier = base_pair(0, earlier)
    summed = summed + block_terms(blocks, middle, grad_x, grad_y)

    def advance_step(position, carried):
        summed, moving, earlier = carried
        moving, rimmed = advance(moving)
        blocks, earlier = base_pair(position, earlier)
        values, slope_x, slope_y = split_rows(rimmed)
        return (summed + block_terms(blocks, values, slope_x, slope_y), moving, earlier)

    summed, moving, earlier = lax.fori_loop(1, groups, advance_step, (summed, moving, earlier))
    return summed


def ceil_to(count, unit):
    return -(-count // unit) * unit


scoped_bytes = 12 * 1024 * 1024
results_flops = 3 * 10**9
fetch_flops = 10**9
hand_on_pieces = 3
in_vmem = pl.BlockSpec(memory_space=pltpu.VMEM)
anywhere = pl.BlockSpec(memory_space=pl.ANY)


def lanes_next(value):
    return pltpu.roll(value, value.shape[1] - 1, 1)


def lanes_before(value):
    return pltpu.roll(value, 1, 1)


def rows_next(value, below):
    count = value.shape[0]
    row = lax.broadcasted_iota(jnp.int32, value.shape, 0)
    return jnp.where(row == count - 1, below, pltpu.roll(value, count - 1, 0))


def rows_before(value, above):
    row = lax.broadcasted_iota(jnp.int32, value.shape, 0)
    return jnp.where(row == 0, above, pltpu.roll(value, 1, 0))


class Sizes:
    def __init__(self, perturbation, groups):
        self.local, _, self.fields, self.width, self.columns = perturbation.shape
        self.groups = groups
        self.total = self.local * groups
        self.components = self.local * 2 * self.fields
        self.edge = ceil_to(self.components + 1, 8)
        cut = self.fields - 1
        self.moved, self.sent = (0, cut), (cut, self.fields)
        self.block_rows = self.local * 2 * (self.fields - cut) * self.width
        self.message_rows = ceil_to(self.block_rows + self.local * 2 * cut * 2, 8)

    def at(self, harmonic, part, field):
        return (harmonic * 2 + part) * self.fields + field

    def block(self, harmonic, part, field):
        first, last = self.sent
        start = ((harmonic * 2 + part) * (last - first) + field - first) * self.width
        return slice(start, start + self.width)

    def rim(self, harmonic, part, field, side):
        first, last = self.moved
        at = ((harmonic * 2 + part) * (last - first) + field - first) * 2 + side
        return slice(self.block_rows + at, self.block_rows + at + 1)

    def shape(self, harmonics, fields):
        return (harmonics, 2, fields[1] - fields[0], self.width, self.columns)

    def each(self):
        for harmonic in range(self.local):
            for part in range(2):
                for field in range(self.fields):
                    yield harmonic, part, field


def edge_rows(sizes, q_ref, visc_ref, row, edge_ref):
    rows = slice(row, row + 1)
    for harmonic, part, field in sizes.each():
        at = sizes.at(harmonic, part, field)
        edge_ref[at : at + 1, :] = q_ref[harmonic, part, field, rows, :]
    at = sizes.components
    edge_ref[at : at + 1, :] = visc_ref[rows, :]
    edge_ref[at + 1 :, :] = jnp.zeros((sizes.edge - at - 1, sizes.columns), jnp.float32)


def visc_kernel(sizes, visc_from, visc_ref, sem):
    copy = pltpu.make_async_copy(visc_from, visc_ref, sem)
    copy.start()
    copy.wait()


def up_kernel(sizes, q_ref, visc_ref, edge_ref):
    edge_rows(sizes, q_ref, visc_ref, sizes.width - 1, edge_ref)


def down_kernel(sizes, q_ref, visc_ref, _, edge_ref):
    edge_rows(sizes, q_ref, visc_ref, 0, edge_ref)


def moved_kernel(sizes, q_ref, moved_ref):
    moved_ref[...] = q_ref[:, :, slice(*sizes.moved)]


def halo(ref, sizes, harmonic, part, field):
    at = sizes.at(harmonic, part, field)
    return halo_rows(ref, sizes, at)


def halo_rows(ref, sizes, at):
    return tuple(ref[start : start + 1, :] for start in (at, sizes.edge + at))


def slope_y(value):
    return 0.5 * (lanes_next(value) - lanes_before(value))


def slope_x(value, above, below):
    return 0.5 * (rows_next(value, below) - rows_before(value, above))


def add_products(sums, chosen, moved):
    real, imag = sums
    for (c_real, c_imag), (m_real, m_imag) in zip(chosen, moved, strict=True):
        more_real = c_real * m_real - c_imag * m_imag
        more_imag = c_real * m_imag + c_imag * m_real
        real = more_real if real is None else real + more_real
        imag = more_imag if imag is None else imag + more_imag
    return real, imag


def chosen_rows(sizes, base, target, source, rows):
    at = lax.rem(target - source + sizes.total, sizes.total)
    return [[base[at, part, term, rows, :] for part in (0, 1)] for term in range(3)]


def chip_sources(sizes):
    me = lax.axis_index("harm")
    return [
        (lax.bitwise_xor(me, place) * sizes.local + harmonic, place, harmonic)
        for place in (0, 1)
        for harmonic in range(sizes.local)
    ]


def far_targets(sizes):
    me = lax.axis_index("harm")
    return [lax.bitwise_xor(me, 2) * sizes.local + harmonic for harmonic in range(sizes.local)]


def block_into(sizes, base, q_own, q_core, block_ref):
    sources = chip_sources(sizes)
    for field in range(*sizes.sent):
        moved = []
        for _, place, harmonic in sources:
            parts = [(q_own, q_core)[place][harmonic, part, field] for part in (0, 1)]
            moved.append(
                [
                    [slope_x(value, 0.0, 0.0) for value in parts],
                    [slope_y(value) for value in parts],
                    parts,
                ]
            )
        for start in range(0, sizes.width, 8):
            rows = slice(start, start + 8)
            for harmonic, target in enumerate(far_targets(sizes)):
                sums = (None, None)
                for terms, (source, _, _) in zip(moved, sources, strict=True):
                    chosen = chosen_rows(sizes, base, target, source, rows)
                    cut = [[value[rows] for value in term] for term in terms]
                    sums = add_products(sums, chosen, cut)
                for part in (0, 1):
                    at = sizes.block(harmonic, part, field).start + start
                    block_ref[at : at + 8, :] = sums[part]


def result_kernel(sizes, base, block_ref, halo_own, halo_core, out_ref):
    out_ref[: sizes.block_rows, :] = block_ref[...]
    sources = chip_sources(sizes)
    for side, row, sign in ((0, 0, -0.5), (1, sizes.width - 1, 0.5)):
        outside = [
            [
                jnp.concatenate(
                    [
                        halo((halo_own, halo_core)[place], sizes, harmonic, part, field)[side]
                        for field in range(sizes.fields)
                    ],
                    axis=0,
                )
                for part in (0, 1)
            ]
            for _, place, harmonic in sources
        ]
        for harmonic, target in enumerate(far_targets(sizes)):
            real = imag = 0.0
            for (q_real, q_imag), (source, _, _) in zip(outside, sources, strict=True):
                at = lax.rem(target - source + sizes.total, sizes.total)
                u_real = sign * base[at, 0, 0, row : row + 1, :]
                u_imag = sign * base[at, 1, 0, row : row + 1, :]
                real = real + u_real * q_real - u_imag * q_imag
                imag = imag + u_real * q_imag + u_imag * q_real
            for part, value in zip((0, 1), (real, imag), strict=True):
                for field in range(sizes.fields):
                    more = value[field : field + 1, :]
                    if field < sizes.moved[1]:
                        out_ref[sizes.rim(harmonic, part, field, side), :] = more
                    else:
                        at = sizes.block(harmonic, part, field).start + row
                        out_ref[at : at + 1, :] += more
    tail = sizes.block_rows + sizes.local * 2 * (sizes.moved[1] - sizes.moved[0]) * 2
    if tail < sizes.message_rows:
        out_ref[tail:, :] = jnp.zeros((sizes.message_rows - tail, sizes.columns), jnp.float32)


def own_terms_into(sizes, q_ref, visc_ref, halo_ref, sum_ref):
    me = lax.axis_index("harm")
    center = visc_ref[...]
    above, below = halo_rows(halo_ref, sizes, sizes.components)
    east = 0.5 * (center + rows_next(center, below))
    west = 0.5 * (center + rows_before(center, above))
    north = 0.5 * (center + lanes_next(center))
    south = 0.5 * (center + lanes_before(center))
    for harmonic in range(sizes.local):
        number = me * sizes.local + harmonic
        signed = jnp.where(number < sizes.total // 2, number, number - sizes.total)
        frequency = omega_base * signed.astype(jnp.float32)
        for part in range(2):
            turn = -frequency if part == 0 else frequency
            terms = {}
            for field in range(sizes.fields):
                value = q_ref[harmonic, part, field]
                above, below = halo(halo_ref, sizes, harmonic, part, field)
                x_next, x_before = rows_next(value, below), rows_before(value, above)
                y_next, y_before = lanes_next(value), lanes_before(value)
                damping = (
                    east * (x_next - value)
                    - west * (value - x_before)
                    + north * (y_next - value)
                    - south * (value - y_before)
                )
                terms[field] = turn * q_ref[harmonic, 1 - part, field] - damping
                if field == 1:
                    dilation = 0.5 * (x_next - x_before)
                elif field == 2:
                    dilation = dilation + 0.5 * (y_next - y_before)
                elif field == 4:
                    terms[1] = terms[1] + 0.5 * (x_next - x_before)
                    terms[2] = terms[2] + 0.5 * (y_next - y_before)
            terms[0] = terms[0] + dilation
            terms[4] = terms[4] + dilation
            for field in range(sizes.fields):
                sum_ref[harmonic, part, field] = terms[field]


def couple(sizes, base, place, fields, start_from, q_ref, halo_ref, slopes, store):
    me = lax.axis_index("harm")
    slopes_x, slopes_y = slopes
    group = lax.bitwise_xor(me, place)
    for field in range(*fields):
        for harmonic in range(sizes.local):
            for part in (0, 1):
                value = q_ref[harmonic, part, field]
                above = below = 0.0
                if halo_ref is not None:
                    above, below = halo(halo_ref, sizes, harmonic, part, field)
                slopes_x[harmonic, part] = slope_x(value, above, below)
                slopes_y[harmonic, part] = slope_y(value)
        for start in range(0, sizes.width, 8):
            rows = slice(start, start + 8)
            sums = [
                [start_from(harmonic, part, field, rows) for part in (0, 1)]
                for harmonic in range(sizes.local)
            ]
            for source in range(sizes.local):
                moved = [
                    [slopes_x[source, part, rows, :] for part in (0, 1)],
                    [slopes_y[source, part, rows, :] for part in (0, 1)],
                    [q_ref[source, part, field, rows, :] for part in (0, 1)],
                ]
                for harmonic in range(sizes.local):
                    target = me * sizes.local + harmonic
                    number = group * sizes.local + source
                    chosen = chosen_rows(sizes, base, target, number, rows)
                    sums[harmonic] = add_products(sums[harmonic], chosen, moved)
            for harmonic in range(sizes.local):
                for part in (0, 1):
                    store(harmonic, part, field, rows, sums[harmonic][part])


def reader(ref):
    return lambda harmonic, part, field, rows: ref[harmonic, part, field, rows, :]


def writer(ref):
    def store(harmonic, part, field, rows, value):
        ref[harmonic, part, field, rows, :] = value

    return store


def block_kernel(sizes, base_a, base_b, base_c, base_d, q_own, q_core, base, block_ref):
    me = lax.axis_index("harm")
    for place, ref in enumerate((base_a, base_b, base_c, base_d)):
        for harmonic in range(sizes.local):
            base[lax.bitwise_xor(me, place) * sizes.local + harmonic] = ref[harmonic]
    block_into(sizes, base, q_own, q_core, block_ref)


def near_kernel(sizes, base, q_own, q_core, halo_own, halo_core, visc_ref, sum_ref, *slopes):
    own_terms_into(sizes, q_own, visc_ref, halo_own, sum_ref)
    everything = (0, sizes.fields)
    for place, q_ref, halo_ref in ((0, q_own, halo_own), (1, q_core, halo_core)):
        couple(
            sizes, base, place, everything, reader(sum_ref), q_ref, halo_ref, slopes, writer(sum_ref)
        )


class Pieces:
    def __init__(self, sizes, refs):
        self.sizes = sizes
        self.blocks = [
            (ref, slice(start, start + 8)) for ref in refs for start in range(0, ref.shape[0], 8)
        ]

    def __getitem__(self, at):
        harmonic, part, field, *rest = at
        plane = (harmonic * 2 + part) * self.sizes.moved[1] + field
        count = self.sizes.width // 8
        chosen = range(rest[0].start // 8, rest[0].stop // 8) if rest else range(count)
        blocks = [self.blocks[plane * count + block] for block in chosen]
        return jnp.concatenate([ref[rows, :] for ref, rows in blocks], axis=0)


def chip_kernel(sizes, base, q_ref, before_ref, sum_ref, *slopes):
    couple(
        sizes, base, 2, sizes.moved, reader(before_ref), q_ref, None, slopes, writer(sum_ref)
    )


def diag_kernel(sizes, base, before_ref, *refs):
    *values, sum_ref, slopes_x, slopes_y = refs
    values, slopes = Pieces(sizes, values), (slopes_x, slopes_y)
    couple(
        sizes, base, 3, sizes.moved, reader(before_ref), values, None, slopes, writer(sum_ref)
    )


def pass_kernel(sizes, values, after, same):
    pass


def sent_kernel(sizes, near_ref, message, _, sum_ref):
    first = sizes.sent[0]
    for field in range(*sizes.sent):
        for harmonic in range(sizes.local):
            for part in (0, 1):
                more = message[sizes.block(harmonic, part, field), :]
                sum_ref[harmonic, part, field - first] = near_ref[harmonic, part, field] + more


def last_kernel(sizes, sent_ref, far_ref, message, out_ref, result, sems):
    copies = []

    def send(source, field):
        copies.append(pltpu.make_async_copy(source, out_ref.at[:, :, field], sems.at[field]))
        copies[-1].start()

    for field in range(*sizes.sent):
        send(sent_ref.at[:, :, field - sizes.sent[0]], field)
    for field in range(*sizes.moved):
        for harmonic in range(sizes.local):
            for part in (0, 1):
                result[harmonic, part, field] = far_ref[harmonic, part, field]
                for side, row in ((0, 0), (1, sizes.width - 1)):
                    more = message[sizes.rim(harmonic, part, field, side), :]
                    result[harmonic, part, field, row : row + 1, :] += more
        send(result.at[:, :, field], field)
    for copy in copies:
        copy.wait()


def paired_shards(perturbation, base_flow, viscosity):
    groups, tiles = lax.axis_size("harm"), lax.axis_size("tile")
    sizes = Sizes(perturbation, groups)

    def to_chip(value):
        return lax.ppermute(value, "harm", [(i, i ^ 2) for i in range(groups)])

    def to_core(value):
        return lax.ppermute(value, "harm", [(i, i ^ 1) for i in range(groups)])

    def along_tile(value, step):
        return lax.ppermute(value, "tile", [(i, (i + step) % tiles) for i in range(tiles)])

    def array(*shape):
        return jax.ShapeDtypeStruct(shape, jnp.float32)

    def call(
        kernel, operands, outs, scratch=(), in_specs=None, out_specs=None, flops=1, aliases=None
    ):
        return pl.pallas_call(
            functools.partial(kernel, sizes),
            in_specs=in_specs or [in_vmem] * len(operands),
            out_shape=outs,
            out_specs=out_specs or [in_vmem] * len(outs),
            scratch_shapes=scratch,
            input_output_aliases=aliases or {},
            cost_estimate=pl.CostEstimate(flops=flops, bytes_accessed=1, transcendentals=0),
            compiler_params=pltpu.CompilerParams(vmem_limit_bytes=scoped_bytes),
        )(*operands)

    slopes = [pltpu.VMEM((sizes.local, 2, sizes.width, sizes.columns), jnp.float32)] * 2
    edges = array(sizes.edge, sizes.columns)

    base_chip = to_chip(base_flow)
    held = perturbation
    visc = call(
        visc_kernel,
        [pltpu.with_memory_space_constraint(viscosity, pltpu.HBM)],
        [array(*viscosity.shape)],
        [pltpu.SemaphoreType.DMA],
        [anywhere],
        flops=fetch_flops,
    )[0]
    up = call(up_kernel, (held, visc), [edges])[0]
    base_core = to_core(base_flow)
    above = along_tile(up, 1)
    moved = call(moved_kernel, (held,), [array(*sizes.shape(sizes.local, sizes.moved))])[0]
    moved_chip = to_chip(moved)
    down = call(
        down_kernel, (held, visc, base_core), [edges], in_specs=[in_vmem] * 2 + [anywhere]
    )[0]
    below = along_tile(down, -1)
    halo_own = jnp.concatenate([above, below], axis=0)
    halo_core = to_core(halo_own)
    held_core = to_core(perturbation)
    base_diag = to_core(base_chip)
    base, block = call(
        block_kernel,
        (base_flow, base_core, base_chip, base_diag, held, held_core),
        [array(sizes.total, *base_flow.shape[1:]), array(sizes.block_rows, sizes.columns)],
    )
    message = call(
        result_kernel,
        (base, block, halo_own, halo_core),
        [array(sizes.message_rows, sizes.columns)],
    )[0]
    results = to_chip(message)
    near_sum = call(
        near_kernel,
        (base, held, held_core, halo_own, halo_core, visc),
        [array(*perturbation.shape)],
        slopes,
    )[0]
    moved_here = call(
        pass_kernel,
        (moved_chip, near_sum),
        array(*moved_chip.shape),
        in_specs=[anywhere] * 2,
        out_specs=anywhere,
        flops=1,
        aliases={0: 0},
    )
    flat = moved_here.reshape(-1, sizes.columns)
    starts = [len(flat) // 8 * place // hand_on_pieces * 8 for place in range(hand_on_pieces + 1)]
    pieces = [to_core(flat[begin:end]) for begin, end in zip(starts, starts[1:])]
    far_sum = call(
        chip_kernel,
        (base, moved_here, near_sum),
        [array(*sizes.shape(sizes.local, sizes.moved))],
        slopes,
    )[0]
    far_sum = call(
        diag_kernel,
        (base, far_sum, *pieces),
        [array(*sizes.shape(sizes.local, sizes.moved))],
        slopes,
    )[0]
    sent_sum = call(
        sent_kernel,
        (near_sum, results, far_sum),
        [array(*sizes.shape(sizes.local, sizes.sent))],
        flops=results_flops,
        in_specs=[in_vmem, in_vmem, anywhere],
    )[0]
    return call(
        last_kernel,
        (sent_sum, far_sum, results),
        array(*perturbation.shape),
        [
            pltpu.VMEM(sizes.shape(sizes.local, sizes.moved), jnp.float32),
            pltpu.SemaphoreType.DMA((sizes.fields,)),
        ],
        out_specs=anywhere,
    )


def solution(mesh):
    placed = (
        P("harm", None, None, ("parts", "tile"), None),
        P("harm", None, None, ("parts", "tile"), None),
        P(("parts", "tile"), None),
    )

    def chosen(perturbation, base_flow, viscosity):
        two_chips = mesh.shape["harm"] == 2 * 2
        whole_tiles = perturbation.shape[3] % 8 == 0 and perturbation.shape[4] % 128 == 0
        body = paired_shards if two_chips and whole_tiles else shards
        return body(perturbation, base_flow, viscosity)

    return jax.shard_map(
        chosen,
        mesh=mesh,
        in_specs=placed,
        out_specs=P("harm", None, None, ("parts", "tile"), None),
        check_vma=False,
    )
```

```python
import functools

import jax
import jax.numpy as jnp
import numpy as np
from jax import lax
from jax.experimental import pallas as pl
from jax.experimental.pallas import tpu as pltpu
from jax.sharding import PartitionSpec as P

omega_base = 0.25


def extended(cells, sides, width):
    for axis, dim in sides:
        count = lax.axis_size(axis)
        head = lax.slice_in_dim(cells, 0, width, axis=dim)
        tail = lax.slice_in_dim(cells, cells.shape[dim] - width, cells.shape[dim], axis=dim)
        cells = jnp.concatenate(
            [
                lax.ppermute(tail, axis, [(i, (i + 1) % count) for i in range(count)]),
                cells,
                lax.ppermute(head, axis, [((i + 1) % count, i) for i in range(count)]),
            ],
            axis=dim,
        )
    return cells


def shifted(value, axis, steps):
    count = lax.axis_size(axis)
    pairs = [(source, (source + steps) % count) for source in range(count)]
    return lax.ppermute(value, axis, pairs)


def split_rows(padded):
    middle = padded[..., 1:-1, :]
    grad_x = 0.5 * (padded[..., 2:, :] - padded[..., :-2, :])
    grad_y = 0.5 * (jnp.roll(middle, -1, -1) - jnp.roll(middle, 1, -1))
    return (middle, grad_x, grad_y)


def diffusion(padded, visc_padded):
    middle = padded[..., 1:-1, :]
    center = visc_padded[1:-1]
    east_face = 0.5 * (center + visc_padded[2:])
    west_face = 0.5 * (center + visc_padded[:-2])
    north_face = 0.5 * (center + jnp.roll(center, -1, -1))
    south_face = 0.5 * (center + jnp.roll(center, 1, -1))
    return (
        east_face * (padded[..., 2:, :] - middle)
        - west_face * (middle - padded[..., :-2, :])
        + north_face * (jnp.roll(middle, -1, -1) - middle)
        - south_face * (middle - jnp.roll(middle, 1, -1))
    )


def acoustic(grad_x, grad_y):
    dilation = grad_x[..., 1, :, :] + grad_y[..., 2, :, :]
    return jnp.stack(
        [dilation, grad_x[..., 4, :, :], grad_y[..., 4, :, :], jnp.zeros_like(dilation), dilation],
        axis=-3,
    )


def own_terms(middle, grad_x, grad_y, damping, frequency):
    rotation = jnp.stack([-frequency * middle[:, 1], frequency * middle[:, 0]], axis=1)
    return rotation + acoustic(grad_x, grad_y) - damping


def coupling(
    u_real, u_imag, v_real, v_imag, g_real, g_imag, q_real, q_imag, x_real, x_imag, y_real, y_imag
):
    real_part = (
        u_real * x_real
        - u_imag * x_imag
        + v_real * y_real
        - v_imag * y_imag
        + g_real * q_real
        - g_imag * q_imag
    )
    imag_part = (
        u_real * x_imag
        + u_imag * x_real
        + v_real * y_imag
        + v_imag * y_real
        + g_real * q_imag
        + g_imag * q_real
    )
    return (real_part, imag_part)


def block_terms(blocks, middle, grad_x, grad_y):
    local_count = middle.shape[0]
    index_table = np.array(
        [
            [local_count + target - source for source in range(local_count)]
            for target in range(local_count)
        ],
        dtype=np.int32,
    )
    chosen = blocks[index_table]

    def base_part(complex_index, field_index):
        return chosen[:, :, complex_index, field_index][:, :, None]

    def moved_part(values, complex_index):
        return values[None, :, complex_index]

    real_part, imag_part = coupling(
        base_part(0, 0),
        base_part(1, 0),
        base_part(0, 1),
        base_part(1, 1),
        base_part(0, 2),
        base_part(1, 2),
        moved_part(middle, 0),
        moved_part(middle, 1),
        moved_part(grad_x, 0),
        moved_part(grad_x, 1),
        moved_part(grad_y, 0),
        moved_part(grad_y, 1),
    )
    return jnp.stack([jnp.sum(real_part, axis=1), jnp.sum(imag_part, axis=1)], axis=1)


def shards(perturbation, base_flow, viscosity):
    local_count = perturbation.shape[0]
    width_x = perturbation.shape[3]
    width_y = perturbation.shape[4]
    groups = lax.axis_size("harm")
    first_index = lax.axis_index("harm") * local_count
    flattened = perturbation.reshape(local_count * 10, width_x, width_y)
    stacked = jnp.concatenate([flattened, viscosity[None]], axis=0)
    padded = extended(stacked, (("tile", 1),), 1)
    own_padded = padded[:-1].reshape(local_count, 2, 5, width_x + 2, width_y)
    visc_padded = padded[-1]
    numbers = first_index + jnp.arange(local_count, dtype=jnp.int32)
    total_count = local_count * groups
    signed = jnp.where(numbers < total_count // 2, numbers, numbers - total_count)
    frequency = (omega_base * signed.astype(jnp.float32)).reshape(local_count, 1, 1, 1)
    middle, grad_x, grad_y = split_rows(own_padded)
    summed = own_terms(middle, grad_x, grad_y, diffusion(own_padded, visc_padded), frequency)
    whole_base = lax.all_gather(base_flow, "harm", axis=0, tiled=True)

    def base_pair(position, earlier):
        before = lax.dynamic_slice_in_dim(
            whole_base, (position + groups - 1) % groups * local_count, local_count, 0
        )
        current = lax.dynamic_slice_in_dim(whole_base, position * local_count, local_count, 0)
        return (jnp.concatenate([before, current], axis=0), earlier)

    earlier = base_flow
    moving = own_padded

    def advance(moving):
        moved = shifted(moving, "harm", 1)
        return (moved, moved)

    blocks, earlier = base_pair(0, earlier)
    summed = summed + block_terms(blocks, middle, grad_x, grad_y)

    def advance_step(position, carried):
        summed, moving, earlier = carried
        moving, rimmed = advance(moving)
        blocks, earlier = base_pair(position, earlier)
        values, slope_x, slope_y = split_rows(rimmed)
        return (summed + block_terms(blocks, values, slope_x, slope_y), moving, earlier)

    summed, moving, earlier = lax.fori_loop(1, groups, advance_step, (summed, moving, earlier))
    return summed


def ceil_to(count, unit):
    return -(-count // unit) * unit


scoped_bytes = 12 * 1024 * 1024
results_flops = 3 * 10**9
hand_on_pieces = 3
in_vmem = pl.BlockSpec(memory_space=pltpu.VMEM)
anywhere = pl.BlockSpec(memory_space=pl.ANY)


def lanes_next(value):
    return pltpu.roll(value, value.shape[1] - 1, 1)


def lanes_before(value):
    return pltpu.roll(value, 1, 1)


def rows_next(value, below):
    count = value.shape[0]
    row = lax.broadcasted_iota(jnp.int32, value.shape, 0)
    return jnp.where(row == count - 1, below, pltpu.roll(value, count - 1, 0))


def rows_before(value, above):
    row = lax.broadcasted_iota(jnp.int32, value.shape, 0)
    return jnp.where(row == 0, above, pltpu.roll(value, 1, 0))


class Sizes:
    def __init__(self, perturbation, groups):
        self.local, _, self.fields, self.width, self.columns = perturbation.shape
        self.groups = groups
        self.total = self.local * groups
        self.components = self.local * 2 * self.fields
        self.edge = ceil_to(self.components + 1, 8)
        cut = self.fields - 1
        self.moved, self.sent = (0, cut), (cut, self.fields)
        self.block_rows = self.local * 2 * (self.fields - cut) * self.width
        self.message_rows = ceil_to(self.block_rows + self.local * 2 * cut * 2, 8)

    def at(self, harmonic, part, field):
        return (harmonic * 2 + part) * self.fields + field

    def block(self, harmonic, part, field):
        first, last = self.sent
        start = ((harmonic * 2 + part) * (last - first) + field - first) * self.width
        return slice(start, start + self.width)

    def rim(self, harmonic, part, field, side):
        first, last = self.moved
        at = ((harmonic * 2 + part) * (last - first) + field - first) * 2 + side
        return slice(self.block_rows + at, self.block_rows + at + 1)

    def shape(self, harmonics, fields):
        return (harmonics, 2, fields[1] - fields[0], self.width, self.columns)

    def each(self):
        for harmonic in range(self.local):
            for part in range(2):
                for field in range(self.fields):
                    yield harmonic, part, field


def fetch_kernel(sizes, q_from, visc_from, q_ref, visc_ref, moved_ref, q_sem, visc_sem):
    copies = (
        pltpu.make_async_copy(q_from, q_ref, q_sem),
        pltpu.make_async_copy(visc_from, visc_ref, visc_sem),
    )
    for copy in copies:
        copy.start()
    for copy in copies:
        copy.wait()
    moved_ref[...] = q_ref[:, :, sizes.moved[0] : sizes.moved[1]]


def edge_kernel(row):
    def kernel(sizes, q_ref, visc_ref, *refs):
        edge_ref = refs[-1]
        rows = slice(row, row + 1) if row >= 0 else slice(sizes.width - 1, sizes.width)
        for harmonic, part, field in sizes.each():
            at = sizes.at(harmonic, part, field)
            edge_ref[at : at + 1, :] = q_ref[harmonic, part, field, rows, :]
        at = sizes.components
        edge_ref[at : at + 1, :] = visc_ref[rows, :]
        edge_ref[at + 1 :, :] = jnp.zeros((sizes.edge - at - 1, sizes.columns), jnp.float32)

    return kernel


def halo(ref, sizes, harmonic, part, field):
    at = sizes.at(harmonic, part, field)
    return halo_rows(ref, sizes, at)


def halo_rows(ref, sizes, at):
    return tuple(ref[start : start + 1, :] for start in (at, sizes.edge + at))


def slope_y(value):
    return 0.5 * (lanes_next(value) - lanes_before(value))


def slope_x(value, above, below):
    return 0.5 * (rows_next(value, below) - rows_before(value, above))


def add_products(sums, chosen, moved):
    real, imag = sums
    for (c_real, c_imag), (m_real, m_imag) in zip(chosen, moved, strict=True):
        more_real = c_real * m_real - c_imag * m_imag
        more_imag = c_real * m_imag + c_imag * m_real
        real = more_real if real is None else real + more_real
        imag = more_imag if imag is None else imag + more_imag
    return real, imag


def chosen_rows(sizes, base, target, source, rows):
    at = lax.rem(target - source + sizes.total, sizes.total)
    return [[base[at, part, term, rows, :] for part in (0, 1)] for term in range(3)]


def chip_sources(sizes):
    me = lax.axis_index("harm")
    return [
        (lax.bitwise_xor(me, place) * sizes.local + harmonic, place, harmonic)
        for place in (0, 1)
        for harmonic in range(sizes.local)
    ]


def far_targets(sizes):
    me = lax.axis_index("harm")
    return [lax.bitwise_xor(me, 2) * sizes.local + harmonic for harmonic in range(sizes.local)]


def block_into(sizes, base, q_own, q_core, block_ref):
    sources = chip_sources(sizes)
    for field in range(*sizes.sent):
        moved = []
        for _, place, harmonic in sources:
            parts = [(q_own, q_core)[place][harmonic, part, field] for part in (0, 1)]
            moved.append(
                [
                    [slope_x(value, 0.0, 0.0) for value in parts],
                    [slope_y(value) for value in parts],
                    parts,
                ]
            )
        for start in range(0, sizes.width, 8):
            rows = slice(start, start + 8)
            for harmonic, target in enumerate(far_targets(sizes)):
                sums = (None, None)
                for terms, (source, _, _) in zip(moved, sources, strict=True):
                    chosen = chosen_rows(sizes, base, target, source, rows)
                    cut = [[value[rows] for value in term] for term in terms]
                    sums = add_products(sums, chosen, cut)
                for part in (0, 1):
                    at = sizes.block(harmonic, part, field).start + start
                    block_ref[at : at + 8, :] = sums[part]


def result_kernel(sizes, base, block_ref, halo_own, halo_core, out_ref):
    out_ref[: sizes.block_rows, :] = block_ref[...]
    sources = chip_sources(sizes)
    for side, row, sign in ((0, 0, -0.5), (1, sizes.width - 1, 0.5)):
        outside = [
            [
                jnp.concatenate(
                    [
                        halo((halo_own, halo_core)[place], sizes, harmonic, part, field)[side]
                        for field in range(sizes.fields)
                    ],
                    axis=0,
                )
                for part in (0, 1)
            ]
            for _, place, harmonic in sources
        ]
        for harmonic, target in enumerate(far_targets(sizes)):
            real = imag = 0.0
            for (q_real, q_imag), (source, _, _) in zip(outside, sources, strict=True):
                at = lax.rem(target - source + sizes.total, sizes.total)
                u_real = sign * base[at, 0, 0, row : row + 1, :]
                u_imag = sign * base[at, 1, 0, row : row + 1, :]
                real = real + u_real * q_real - u_imag * q_imag
                imag = imag + u_real * q_imag + u_imag * q_real
            for part, value in zip((0, 1), (real, imag), strict=True):
                for field in range(sizes.fields):
                    more = value[field : field + 1, :]
                    if field < sizes.moved[1]:
                        out_ref[sizes.rim(harmonic, part, field, side), :] = more
                    else:
                        at = sizes.block(harmonic, part, field).start + row
                        out_ref[at : at + 1, :] += more
    tail = sizes.block_rows + sizes.local * 2 * (sizes.moved[1] - sizes.moved[0]) * 2
    if tail < sizes.message_rows:
        out_ref[tail:, :] = jnp.zeros((sizes.message_rows - tail, sizes.columns), jnp.float32)


def own_terms_into(sizes, q_ref, visc_ref, halo_ref, sum_ref):
    me = lax.axis_index("harm")
    center = visc_ref[...]
    above, below = halo_rows(halo_ref, sizes, sizes.components)
    east = 0.5 * (center + rows_next(center, below))
    west = 0.5 * (center + rows_before(center, above))
    north = 0.5 * (center + lanes_next(center))
    south = 0.5 * (center + lanes_before(center))
    for harmonic in range(sizes.local):
        number = me * sizes.local + harmonic
        signed = jnp.where(number < sizes.total // 2, number, number - sizes.total)
        frequency = omega_base * signed.astype(jnp.float32)
        for part in range(2):
            turn = -frequency if part == 0 else frequency
            terms = {}
            for field in range(sizes.fields):
                value = q_ref[harmonic, part, field]
                above, below = halo(halo_ref, sizes, harmonic, part, field)
                x_next, x_before = rows_next(value, below), rows_before(value, above)
                y_next, y_before = lanes_next(value), lanes_before(value)
                damping = (
                    east * (x_next - value)
                    - west * (value - x_before)
                    + north * (y_next - value)
                    - south * (value - y_before)
                )
                terms[field] = turn * q_ref[harmonic, 1 - part, field] - damping
                if field == 1:
                    dilation = 0.5 * (x_next - x_before)
                elif field == 2:
                    dilation = dilation + 0.5 * (y_next - y_before)
                elif field == 4:
                    terms[1] = terms[1] + 0.5 * (x_next - x_before)
                    terms[2] = terms[2] + 0.5 * (y_next - y_before)
            terms[0] = terms[0] + dilation
            terms[4] = terms[4] + dilation
            for field in range(sizes.fields):
                sum_ref[harmonic, part, field] = terms[field]


def couple(sizes, base, place, fields, start_from, q_ref, halo_ref, slopes, store):
    me = lax.axis_index("harm")
    slopes_x, slopes_y = slopes
    group = lax.bitwise_xor(me, place)
    for field in range(*fields):
        for harmonic in range(sizes.local):
            for part in (0, 1):
                value = q_ref[harmonic, part, field]
                above = below = 0.0
                if halo_ref is not None:
                    above, below = halo(halo_ref, sizes, harmonic, part, field)
                slopes_x[harmonic, part] = slope_x(value, above, below)
                slopes_y[harmonic, part] = slope_y(value)
        for start in range(0, sizes.width, 8):
            rows = slice(start, start + 8)
            sums = [
                [start_from(harmonic, part, field, rows) for part in (0, 1)]
                for harmonic in range(sizes.local)
            ]
            for source in range(sizes.local):
                moved = [
                    [slopes_x[source, part, rows, :] for part in (0, 1)],
                    [slopes_y[source, part, rows, :] for part in (0, 1)],
                    [q_ref[source, part, field, rows, :] for part in (0, 1)],
                ]
                for harmonic in range(sizes.local):
                    target = me * sizes.local + harmonic
                    number = group * sizes.local + source
                    chosen = chosen_rows(sizes, base, target, number, rows)
                    sums[harmonic] = add_products(sums[harmonic], chosen, moved)
            for harmonic in range(sizes.local):
                for part in (0, 1):
                    store(harmonic, part, field, rows, sums[harmonic][part])


def reader(ref):
    return lambda harmonic, part, field, rows: ref[harmonic, part, field, rows, :]


def writer(ref):
    def store(harmonic, part, field, rows, value):
        ref[harmonic, part, field, rows, :] = value

    return store


def own_kernel(
    sizes, base_a, base_b, base_c, base_d, q_own, q_core, halo_ref, visc_ref, sum_ref, base, block_ref,
    *slopes,
):
    me = lax.axis_index("harm")
    for place, ref in enumerate((base_a, base_b, base_c, base_d)):
        for harmonic in range(sizes.local):
            base[lax.bitwise_xor(me, place) * sizes.local + harmonic] = ref[harmonic]
    block_into(sizes, base, q_own, q_core, block_ref)
    own_terms_into(sizes, q_own, visc_ref, halo_ref, sum_ref)
    everything = (0, sizes.fields)
    couple(sizes, base, 0, everything, reader(sum_ref), q_own, halo_ref, slopes, writer(sum_ref))


def core_kernel(sizes, base, q_ref, halo_ref, before_ref, sum_ref, *slopes):
    everything = (0, sizes.fields)
    couple(sizes, base, 1, everything, reader(before_ref), q_ref, halo_ref, slopes, writer(sum_ref))


class Pieces:
    def __init__(self, sizes, refs):
        self.sizes = sizes
        self.blocks = [
            (ref, slice(start, start + 8)) for ref in refs for start in range(0, ref.shape[0], 8)
        ]

    def __getitem__(self, at):
        harmonic, part, field, *rest = at
        plane = (harmonic * 2 + part) * self.sizes.moved[1] + field
        count = self.sizes.width // 8
        chosen = range(rest[0].start // 8, rest[0].stop // 8) if rest else range(count)
        blocks = [self.blocks[plane * count + block] for block in chosen]
        return jnp.concatenate([ref[rows, :] for ref, rows in blocks], axis=0)


def chip_kernel(sizes, base, q_ref, before_ref, sum_ref, *slopes):
    couple(
        sizes, base, 2, sizes.moved, reader(before_ref), q_ref, None, slopes, writer(sum_ref)
    )


def diag_kernel(sizes, base, before_ref, *refs):
    *values, sum_ref, slopes_x, slopes_y = refs
    values, slopes = Pieces(sizes, values), (slopes_x, slopes_y)
    couple(
        sizes, base, 3, sizes.moved, reader(before_ref), values, None, slopes, writer(sum_ref)
    )


def pass_kernel(sizes, values, after, same):
    pass


def sent_kernel(sizes, near_ref, message, _, sum_ref):
    first = sizes.sent[0]
    for field in range(*sizes.sent):
        for harmonic in range(sizes.local):
            for part in (0, 1):
                more = message[sizes.block(harmonic, part, field), :]
                sum_ref[harmonic, part, field - first] = near_ref[harmonic, part, field] + more


def last_kernel(sizes, sent_ref, far_ref, message, out_ref, result, sems):
    copies = []

    def send(source, field):
        copies.append(pltpu.make_async_copy(source, out_ref.at[:, :, field], sems.at[field]))
        copies[-1].start()

    for field in range(*sizes.sent):
        send(sent_ref.at[:, :, field - sizes.sent[0]], field)
    for field in range(*sizes.moved):
        for harmonic in range(sizes.local):
            for part in (0, 1):
                result[harmonic, part, field] = far_ref[harmonic, part, field]
                for side, row in ((0, 0), (1, sizes.width - 1)):
                    more = message[sizes.rim(harmonic, part, field, side), :]
                    result[harmonic, part, field, row : row + 1, :] += more
        send(result.at[:, :, field], field)
    for copy in copies:
        copy.wait()


def paired_shards(perturbation, base_flow, viscosity):
    groups, tiles = lax.axis_size("harm"), lax.axis_size("tile")
    sizes = Sizes(perturbation, groups)

    def to_chip(value):
        return lax.ppermute(value, "harm", [(i, i ^ 2) for i in range(groups)])

    def to_core(value):
        return lax.ppermute(value, "harm", [(i, i ^ 1) for i in range(groups)])

    def along_tile(value, step):
        return lax.ppermute(value, "tile", [(i, (i + step) % tiles) for i in range(tiles)])

    def array(*shape):
        return jax.ShapeDtypeStruct(shape, jnp.float32)

    def call(
        kernel, operands, outs, scratch=(), in_specs=None, out_specs=None, flops=1, aliases=None
    ):
        return pl.pallas_call(
            functools.partial(kernel, sizes),
            in_specs=in_specs or [in_vmem] * len(operands),
            out_shape=outs,
            out_specs=out_specs or [in_vmem] * len(outs),
            scratch_shapes=scratch,
            input_output_aliases=aliases or {},
            cost_estimate=pl.CostEstimate(flops=flops, bytes_accessed=1, transcendentals=0),
            compiler_params=pltpu.CompilerParams(vmem_limit_bytes=scoped_bytes),
        )(*operands)

    slopes = [pltpu.VMEM((sizes.local, 2, sizes.width, sizes.columns), jnp.float32)] * 2
    edges = array(sizes.edge, sizes.columns)

    base_chip = to_chip(base_flow)
    held, visc, moved = call(
        fetch_kernel,
        [pltpu.with_memory_space_constraint(x, pltpu.HBM) for x in (perturbation, viscosity)],
        [
            array(*perturbation.shape),
            array(*viscosity.shape),
            array(*sizes.shape(sizes.local, sizes.moved)),
        ],
        [pltpu.SemaphoreType.DMA] * 2,
        [anywhere] * 2,
    )
    up = call(edge_kernel(-1), (held, visc), [edges])[0]
    base_core = to_core(base_flow)
    above = along_tile(up, 1)
    moved_chip = to_chip(moved)
    down = call(
        edge_kernel(0), (held, visc, base_core), [edges], in_specs=[in_vmem] * 2 + [anywhere]
    )[0]
    below = along_tile(down, -1)
    halo_own = jnp.concatenate([above, below], axis=0)
    halo_core = to_core(halo_own)
    held_core = to_core(perturbation)
    base_diag = to_core(base_chip)
    own_sum, base, block = call(
        own_kernel,
        (base_flow, base_core, base_chip, base_diag, held, held_core, halo_own, visc),
        [
            array(*perturbation.shape),
            array(sizes.total, *base_flow.shape[1:]),
            array(sizes.block_rows, sizes.columns),
        ],
        slopes,
    )
    message = call(
        result_kernel,
        (base, block, halo_own, halo_core),
        [array(sizes.message_rows, sizes.columns)],
    )[0]
    results = to_chip(message)
    near_sum = call(
        core_kernel, (base, held_core, halo_core, own_sum), [array(*perturbation.shape)], slopes
    )[0]
    moved_here = call(
        pass_kernel,
        (moved_chip, message),
        array(*moved_chip.shape),
        in_specs=[anywhere] * 2,
        out_specs=anywhere,
        flops=1,
        aliases={0: 0},
    )
    flat = moved_here.reshape(-1, sizes.columns)
    starts = [len(flat) // 8 * place // hand_on_pieces * 8 for place in range(hand_on_pieces + 1)]
    pieces = [to_core(flat[begin:end]) for begin, end in zip(starts, starts[1:])]
    far_sum = call(
        chip_kernel,
        (base, moved_here, near_sum),
        [array(*sizes.shape(sizes.local, sizes.moved))],
        slopes,
    )[0]
    far_sum = call(
        diag_kernel,
        (base, far_sum, *pieces),
        [array(*sizes.shape(sizes.local, sizes.moved))],
        slopes,
    )[0]
    sent_sum = call(
        sent_kernel,
        (near_sum, results, far_sum),
        [array(*sizes.shape(sizes.local, sizes.sent))],
        flops=results_flops,
        in_specs=[in_vmem, in_vmem, anywhere],
    )[0]
    return call(
        last_kernel,
        (sent_sum, far_sum, results),
        array(*perturbation.shape),
        [
            pltpu.VMEM(sizes.shape(sizes.local, sizes.moved), jnp.float32),
            pltpu.SemaphoreType.DMA((sizes.fields,)),
        ],
        out_specs=anywhere,
    )


def solution(mesh):
    placed = (
        P("harm", None, None, ("parts", "tile"), None),
        P("harm", None, None, ("parts", "tile"), None),
        P(("parts", "tile"), None),
    )

    def chosen(perturbation, base_flow, viscosity):
        two_chips = mesh.shape["harm"] == 2 * 2
        whole_tiles = perturbation.shape[3] % 8 == 0 and perturbation.shape[4] % 128 == 0
        body = paired_shards if two_chips and whole_tiles else shards
        return body(perturbation, base_flow, viscosity)

    return jax.shard_map(
        chosen,
        mesh=mesh,
        in_specs=placed,
        out_specs=P("harm", None, None, ("parts", "tile"), None),
        check_vma=False,
    )
```
